512 devices in a mesh: dp: 4 (over y_lo), seq: 32 (over z, x), head: 4 (over y_hi, core).
Axes of the slice: x: 4, y: 8 (y_hi: 2, y_lo: 4; y = y_hi * 4 + y_lo), z: 8, core: 2. Of those that a mesh axis runs over, the one named last changes fastest.
Arguments:
- queries: bfloat16 [28672, 1024], P(('dp', 'seq', 'head')), parts along dimension 0, may hold values from -6 to 6
- key_rows: bfloat16 [28672, 1024], P(('dp', 'seq', 'head')), parts along dimension 0, may hold values from -6 to 6
- values: bfloat16 [28672, 1024], P(('dp', 'seq', 'head')), parts along dimension 0, may hold values from -6 to 6
- query_tangent: bfloat16 [28672, 1024], P(('dp', 'seq', 'head')), parts along dimension 0, may hold values from -6 to 6
- key_tangent: bfloat16 [28672, 1024], P(('dp', 'seq', 'head')), parts along dimension 0, may hold values from -6 to 6
- value_tangent: bfloat16 [28672, 1024], P(('dp', 'seq', 'head')), parts along dimension 0, may hold values from -6 to 6
- out_weight: bfloat16 [1024, 1536], replicated, may hold values from -4 to 4
- gate_vector: float32 [6144], P('dp'), parts along dimension 0, may hold values from 0.1 to 1.9
- gate_tangent: float32 [6144], P('dp'), parts along dimension 0, may hold values from -6 to 6
Outputs:
- block_out: bfloat16 [28672, 1536], P(('dp', 'seq', 'head')), parts along dimension 0
- block_tangent: bfloat16 [28672, 1536], P(('dp', 'seq', 'head')), parts along dimension 0
The draws below stay inside these ranges and needn't reach their ends.
There are 4 independent parts, one for each index of `dp`. The reference program is written for one: setup_inputs(seed, part) draws one part's arguments, and reference() takes and returns one part's arrays. A program takes and returns all parts, laid end to end along the dimension named above; an argument that names none is the same for every part. Nothing has to cross between parts.
All inputs are finite; a program needn't handle non-finite values.
Results may differ from the reference program's by a relative error of at most 0.014.
Values may be sent and summed in bfloat16 or wider, within the bound.
A program may use at most 64 MiB of HBM per device.

```python
import jax
import jax.numpy as jnp
from jax import lax

D = 1536
HEADS = 8
HD = 128
TOKENS = 7168


def draw_queries(key, part):
    key = jax.random.fold_in(key, 1)
    base_draw = jnp.clip(1.2 * jax.random.normal(key, (TOKENS, HEADS * HD), jnp.float32), -6.0, 6.0)
    return base_draw.astype(jnp.bfloat16)


def draw_key_rows(key, part):
    key = jax.random.fold_in(key, 2)
    base_draw = jnp.clip(1.2 * jax.random.normal(key, (TOKENS, HEADS * HD), jnp.float32), -6.0, 6.0)
    return base_draw.astype(jnp.bfloat16)


def shard_levels(own_key, dims, pieces, low, largest):
    def one(axis_at, blocks):
        steps = jax.random.uniform(jax.random.fold_in(jax.random.fold_in(own_key, 6), axis_at), (blocks,), jnp.float32, low / len(pieces), largest / len(pieces))
        return jnp.repeat(jnp.exp(steps), dims[axis_at] // blocks).reshape((-1,) + (1,) * (len(dims) - axis_at - 1))

    factor_of = one(*pieces[0])
    for cut in pieces[1:]:
        factor_of = factor_of * one(*cut)
    return factor_of


def centred(own_key, shape, width, limit, pieces=(), dtype=jnp.bfloat16):
    values = jax.random.normal(own_key, shape, jnp.float32) * width
    if len(pieces) > 0:
        values = shard_levels(own_key, shape, pieces, -0.22, 0.18) * values
    return jnp.clip(values, min=-limit, max=limit).astype(dtype)


def setup_inputs(seed: int = 0, part: int = 0) -> dict:
    streams_of = jax.random.split(jax.random.key(seed), 10)
    own_keys = jax.random.split(jax.random.fold_in(streams_of[9], part), 10)
    return {
        "queries": draw_queries(jax.random.fold_in(jax.random.fold_in(streams_of[9], part), 71), part),
        "key_rows": draw_key_rows(jax.random.fold_in(jax.random.fold_in(streams_of[9], part), 71), part),
        "values": centred(own_keys[2], (TOKENS, HEADS * HD), 1.0, 6.0, ((0, 128),)),
        "query_tangent": centred(own_keys[3], (TOKENS, HEADS * HD), 1.0, 6.0, ((0, 128),)),
        "key_tangent": centred(own_keys[4], (TOKENS, HEADS * HD), 1.0, 6.0, ((0, 128),)),
        "value_tangent": centred(own_keys[5], (TOKENS, HEADS * HD), 1.0, 6.0, ((0, 128),)),
        "out_weight": centred(streams_of[6], (HEADS * HD, D), (HEADS * HD * 16 // TOKENS) ** -0.5, 4.0),
        "gate_vector": jnp.clip(1.0 + 0.18 * jax.random.normal(own_keys[7], (D,), jnp.float32), 0.1, 1.9),
        "gate_tangent": centred(own_keys[8], (D,), 1.0, 6.0, (), jnp.float32),
    }


def head_attention(operands):
    query_head, key_head, value_head, query_dot, key_dot, value_dot = operands
    score_scale = HD ** -0.5
    scores = jnp.dot(query_head, key_head.T, preferred_element_type=jnp.float32) * score_scale
    score_tangent = (jnp.dot(query_dot, key_head.T, preferred_element_type=jnp.float32)
                     + jnp.dot(query_head, key_dot.T, preferred_element_type=jnp.float32)) * score_scale
    row_max = jnp.max(scores, axis=-1, keepdims=True)
    weights = jnp.exp(scores - row_max).astype(jnp.bfloat16)
    weight_wide = weights.astype(jnp.float32)
    shifted = weight_wide * score_tangent
    row_total = jnp.sum(weight_wide, axis=-1, keepdims=True)
    tilt_sum = jnp.sum(shifted, axis=-1, keepdims=True)
    shaded = shifted.astype(jnp.bfloat16)
    weighted = jnp.dot(weights, value_head, preferred_element_type=jnp.float32)
    tangent_acc = (jnp.dot(weights, value_dot, preferred_element_type=jnp.float32)
                   + jnp.dot(shaded, value_head, preferred_element_type=jnp.float32))
    attended = weighted / row_total
    attended_tangent = tangent_acc / row_total - (tilt_sum / row_total) * attended
    return attended.astype(jnp.bfloat16), attended_tangent.astype(jnp.bfloat16)


def by_head(matrix):
    return matrix.reshape(TOKENS, HEADS, HD).transpose(1, 0, 2)


def reference(queries, key_rows, values, query_tangent, key_tangent, value_tangent, out_weight, gate_vector, gate_tangent):
    operands = tuple(by_head(member) for member in (queries, key_rows, values, query_tangent, key_tangent, value_tangent))
    attended, attended_tangent = lax.map(head_attention, operands)
    attended = attended.transpose(1, 0, 2).reshape(TOKENS, HEADS * HD)
    attended_tangent = attended_tangent.transpose(1, 0, 2).reshape(TOKENS, HEADS * HD)
    projected = jnp.dot(attended, out_weight, preferred_element_type=jnp.float32)
    projected_tangent = jnp.dot(attended_tangent, out_weight, preferred_element_type=jnp.float32)
    block_out = (gate_vector * projected).astype(jnp.bfloat16)
    block_tangent = (gate_tangent * projected + gate_vector * projected_tangent).astype(jnp.bfloat16)
    return block_out, block_tangent
```

```python
import functools

import jax
import jax.numpy as jnp
from jax import lax
from jax.experimental import pallas as pl
from jax.experimental.pallas import tpu as pltpu
from jax.sharding import PartitionSpec as P

HD = 128
VMEM_LIMIT = 64 * 1024 * 1024
MESH = pl.DeviceIdType.MESH
SCALE = HD**-0.5
LOG2E = 1.4426950408889634
F32 = jnp.float32
BF16 = jnp.bfloat16
NEAR, FAR = 0, 1
LEFTWARD, RIGHTWARD = 0, 1


def kernel(
    nx,
    nz,
    q_hbm,
    k_hbm,
    v_hbm,
    qd_hbm,
    kd_hbm,
    vd_hbm,
    w_hbm,
    gate_hbm,
    gate_dot_hbm,
    out_ref,
    out_dot_ref,
    staged,
    gates,
    send_kv,
    send_q,
    land_kv,
    land_q,
    kv,
    q_all,
    acc,
    acc_shaded,
    row_max,
    row_total,
    tilt_sum,
    out_send,
    out_land,
    weight,
    staged_sems,
    gate_sems,
    weight_sem,
    kv_sems,
    q_sems,
    out_sems,
    ring_send_sems,
    ring_recv_sems,
    pair_send_sems,
    pair_recv_sems,
):
    tokens = q_hbm.shape[0]
    group = 2 * nx
    far_rows = nx * tokens
    half = nz // 2
    dp = lax.axis_index("dp")
    seq = lax.axis_index("seq")
    head_axis = lax.axis_index("head")
    z, x = seq // nx, seq % nx
    y, core = head_axis // 2, head_axis % 2

    def device(z_at, y_at, x_at, core_at):
        return (dp, z_at * nx + x_at, y_at * 2 + core_at)

    def taker(j):
        return device(z, (y + j // nx) % 2, (x + j % nx) % nx, core)

    def giver(j):
        return device(z, (y + j // nx) % 2, (x + nx - j % nx) % nx, core)

    def head_of(j):
        return ((y + j // nx) % 2) * nx + (x + j % nx) % nx

    right = device((z + 1) % nz, y, x, core)
    left = device((z + nz - 1) % nz, y, x, core)
    sibling = device(z, y, x, 1 - core)

    staged_copies = [
        pltpu.make_async_copy(ref, staged.at[i], staged_sems.at[i])
        for i, ref in enumerate((k_hbm, kd_hbm, v_hbm, vd_hbm, q_hbm, qd_hbm))
    ]
    for copy in staged_copies:
        copy.start()
    weight_copies = [
        pltpu.make_async_copy(gate_hbm, gates.at[0, 0], gate_sems.at[0]),
        pltpu.make_async_copy(gate_dot_hbm, gates.at[1, 0], gate_sems.at[1]),
    ]
    for copy in weight_copies:
        copy.start()
    for j in range(group):
        rows = pl.ds(pl.multiple_of(head_of(j) * HD, HD), HD)
        copy = pltpu.make_async_copy(
            w_hbm.at[rows], weight.at[pl.ds(j * HD, HD)], weight_sem.at[j]
        )
        copy.start()
        weight_copies.append(copy)

    barrier = pltpu.get_barrier_semaphore()
    partners = [taker(j) for j in range(1, group)] + [sibling, right]
    if nz > 2:
        partners.append(left)
    for partner in partners:
        pl.semaphore_signal(barrier, inc=1, device_id=partner, device_id_type=MESH)

    for copy in staged_copies:
        copy.wait()
    for j in range(group):
        columns = pl.ds(pl.multiple_of(head_of(j) * HD, HD), HD)
        send_kv[j] = jnp.concatenate(
            [staged[i, :, columns].astype(F32) for i in range(4)], axis=0
        ).astype(BF16)
        send_q[j] = jnp.concatenate(
            [staged[i, :, columns].astype(F32) for i in (4, 5)], axis=0
        ).astype(BF16)

    pl.semaphore_wait(barrier, len(partners))

    def remote(src, dst, send_sem, recv_sem, to):
        return pltpu.make_async_remote_copy(
            src_ref=src,
            dst_ref=dst,
            send_sem=send_sem,
            recv_sem=recv_sem,
            device_id=to,
            device_id_type=MESH,
        )

    kv_copies = [
        None
        if j == 0
        else remote(send_kv.at[j], land_kv.at[j], kv_sems.at[0, j], kv_sems.at[1, j], taker(j))
        for j in range(group)
    ]
    q_copies = [
        None
        if j == 0
        else remote(send_q.at[j], land_q.at[j], q_sems.at[0, j], q_sems.at[1, j], taker(j))
        for j in range(group)
    ]
    for j in range(1, nx):
        kv_copies[j].start()
    for j in range(nx, group):
        q_copies[j].start()
        kv_copies[j].start()
    for j in range(1, nx):
        q_copies[j].start()

    def slot(way, step):
        if step == 0:
            return half - 1, 0
        if step == half:
            return half - 1, 1
        return step - 1, way

    def steps_of(piece, way):
        return half if (piece == NEAR) == (way == RIGHTWARD) else half - 1

    ring_copies = {}
    pair_copies = {}
    for piece in (NEAR, FAR):
        for way in (LEFTWARD, RIGHTWARD):
            for step in range(1, steps_of(piece, way) + 1):
                for part in (0, 1):
                    from_p, from_sub = slot(way, step - 1)
                    to_p, to_sub = slot(way, step)
                    ring_copies[piece, way, step, part] = remote(
                        kv.at[piece, from_p, part, from_sub],
                        kv.at[piece, to_p, part, to_sub],
                        ring_send_sems.at[piece, way, step - 1, part],
                        ring_recv_sems.at[piece, way, step - 1, part],
                        right if way == RIGHTWARD else left,
                    )
        for p in range(half):
            for sub in (0, 1):
                for part in (0, 1):
                    pair_copies[piece, p, sub, part] = remote(
                        kv.at[piece, p, part, sub],
                        kv.at[piece, p, part, 2 + sub],
                        pair_send_sems.at[piece, p, sub, part],
                        pair_recv_sems.at[piece, p, sub, part],
                        sibling,
                    )

    def start_piece(piece):
        members = range(piece * nx, (piece + 1) * nx)
        for j in members:
            if j > 0:
                kv_copies[j].wait_recv()
        blocks = [(send_kv if j == 0 else land_kv)[j].astype(F32) for j in members]
        for part in (0, 1):
            for side in (0, 1):
                at = (2 * part + side) * tokens
                kv[piece, half - 1, part, 0, :, side * HD : (side + 1) * HD] = jnp.concatenate(
                    [block[at : at + tokens] for block in blocks], axis=0
                ).astype(BF16)
        for part in (0, 1):
            for way in (RIGHTWARD, LEFTWARD):
                if steps_of(piece, way) >= 1:
                    ring_copies[piece, way, 1, part].start()
        for part in (0, 1):
            pair_copies[piece, half - 1, 0, part].start()

    def pass_on(piece, step):
        for part in (0, 1):
            for way in (RIGHTWARD, LEFTWARD):
                if step <= steps_of(piece, way):
                    ring_copies[piece, way, step, part].wait_recv()
                    if step + 1 <= steps_of(piece, way):
                        ring_copies[piece, way, step + 1, part].start()
                    p, sub = slot(way, step)
                    pair_copies[piece, p, sub, part].start()

    def gather_queries():
        if gathered:
            return
        gathered.append(True)
        for j in range(1, group):
            q_copies[j].wait_recv()
        for side, at in ((0, tokens), (1, 0)):
            q_all[:, side * HD : (side + 1) * HD] = jnp.concatenate(
                [
                    (send_q if j == 0 else land_q)[j].astype(F32)[at : at + tokens]
                    for j in range(group)
                ],
                axis=0,
            ).astype(BF16)

    def absorb(piece, p, chunk):
        rows = pl.ds(pl.multiple_of(chunk * far_rows, 8), far_rows)
        query_rows = pl.ds(pl.multiple_of(chunk * far_rows, 16), far_rows)
        keys = kv[piece, p, 0].reshape(4 * far_rows, 2 * HD)
        vals = kv[piece, p, 1].reshape(4 * far_rows, 2 * HD)
        both = q_all[query_rows, :]
        transposed = (((1,), (1,)), ((), ()))
        scores = lax.dot_general(
            both[:, HD:], keys[:, :HD], transposed, preferred_element_type=F32
        ) * (SCALE * LOG2E)
        score_tangent = lax.dot_general(both, keys, transposed, preferred_element_type=F32)
        max_was = row_max[rows, :][:, :1]
        max_now = jnp.maximum(max_was, jnp.max(scores, axis=-1, keepdims=True))
        rescale = jnp.exp2(max_was - max_now)
        weights = jnp.exp2(scores - max_now).astype(BF16)
        wide = weights.astype(F32)
        shifted = wide * score_tangent
        shaded = shifted.astype(BF16)
        row_max[rows, :] = jnp.broadcast_to(max_now, (far_rows, HD))
        row_total[rows, :] = row_total[rows, :] * rescale + jnp.sum(wide, axis=-1, keepdims=True)
        tilt_sum[rows, :] = tilt_sum[rows, :] * rescale + jnp.sum(shifted, axis=-1, keepdims=True)
        acc[rows, :] = acc[rows, :] * rescale + jnp.dot(weights, vals, preferred_element_type=F32)
        acc_shaded[rows, :] = acc_shaded[rows, :] * rescale + jnp.dot(
            shaded, vals[:, :HD], preferred_element_type=F32
        )

    def absorb_all(piece, p):
        for sub in (0, 1):
            for part in (0, 1):
                pair_copies[piece, p, sub, part].wait_recv()

        def one(chunk, carry):
            absorb(piece, p, chunk)
            return carry

        lax.fori_loop(0, 2, one, 0)

    row_max[...] = jnp.full(row_max.shape, -1e30, F32)
    row_total[...] = jnp.zeros(row_total.shape, F32)
    tilt_sum[...] = jnp.zeros(tilt_sum.shape, F32)
    acc[...] = jnp.zeros(acc.shape, F32)
    acc_shaded[...] = jnp.zeros(acc_shaded.shape, F32)

    start_piece(NEAR)
    order = [(NEAR, step) for step in range(1, min(half, 2) + 1)] + [(FAR, 0)]
    near_left = [(NEAR, step) for step in range(3, half + 1)]
    far_left = [(FAR, step) for step in range(1, half + 1)]
    while near_left or far_left:
        if near_left:
            order.append(near_left.pop(0))
        if far_left:
            order.append(far_left.pop(0))
    ready = []
    gathered = []
    for at, (piece, step) in enumerate(order):
        last = at == len(order) - 1
        if last:
            gather_queries()
            while ready:
                absorb_all(*ready.pop(0))
        if step == 0:
            start_piece(piece)
            continue
        pass_on(piece, step)
        if ready and not last:
            gather_queries()
            absorb_all(*ready.pop(0))
        ready.append((piece, step - 1))

    (piece, p), = ready
    for sub in (0, 1):
        for part in (0, 1):
            pair_copies[piece, p, sub, part].wait_recv()
    out_copies = [
        None
        if j == 0
        else remote(out_send.at[j], out_land.at[j], out_sems.at[0, j], out_sems.at[1, j], giver(j))
        for j in range(group)
    ]
    for chunk in (1, 0):
        absorb(piece, p, chunk)
        rows = slice(chunk * far_rows, (chunk + 1) * far_rows)
        inverse = 1.0 / row_total[rows, :]
        attended = acc[rows, :HD] * inverse
        tangent = acc[rows, HD:] + SCALE * acc_shaded[rows, :]
        attended_dot = tangent * inverse - (SCALE * tilt_sum[rows, :] * inverse) * attended
        for at in range(nx):
            j = chunk * nx + at
            own = slice(at * tokens, (at + 1) * tokens)
            block = jnp.concatenate([attended[own], attended_dot[own]], axis=0).astype(BF16)
            if j == 0:
                out_land[j] = block
            else:
                out_send[j] = block
                out_copies[j].start()

    for copy in weight_copies:
        copy.wait()
    for j in range(1, group):
        out_copies[j].wait_recv()
    everything = jnp.concatenate([out_land[j] for j in range(group)], axis=1)
    projected = jnp.dot(everything, weight[...], preferred_element_type=F32)
    primal, dot = projected[:tokens], projected[tokens:]
    gate, gate_dot = gates[0], gates[1]
    out_ref[...] = (gate * primal).astype(BF16)
    out_dot_ref[...] = (gate_dot * primal + gate * dot).astype(BF16)

    for j in range(1, group):
        kv_copies[j].wait_send()
        q_copies[j].wait_send()
        out_copies[j].wait_send()
    for copy in ring_copies.values():
        copy.wait_send()
    for copy in pair_copies.values():
        copy.wait_send()


def local(
    queries,
    key_rows,
    values,
    query_tangent,
    key_tangent,
    value_tangent,
    out_weight,
    gate_vector,
    gate_tangent,
    *,
    seq_size,
):
    tokens = queries.shape[0]
    group = queries.shape[1] // HD
    nx = group // 2
    nz = seq_size // nx
    width = out_weight.shape[1]
    rows = group * tokens
    piece_rows = nx * tokens
    half = nz // 2
    vmem = pl.BlockSpec(memory_space=pltpu.VMEM)
    out_shape = jax.ShapeDtypeStruct((tokens, width), BF16)
    all_rows = rows * nz * 2
    return pl.pallas_call(
        functools.partial(kernel, nx, nz),
        out_shape=(out_shape, out_shape),
        in_specs=[pl.BlockSpec(memory_space=pl.ANY)] * 9,
        out_specs=(vmem, vmem),
        scratch_shapes=[
            pltpu.VMEM((6, tokens, group * HD), BF16),
            pltpu.VMEM((2, 1, width), F32),
            pltpu.VMEM((group, 4 * tokens, HD), BF16),
            pltpu.VMEM((group, 2 * tokens, HD), BF16),
            pltpu.VMEM((group, 4 * tokens, HD), BF16),
            pltpu.VMEM((group, 2 * tokens, HD), BF16),
            pltpu.VMEM((2, half, 2, 4, piece_rows, 2 * HD), BF16),
            pltpu.VMEM((rows, 2 * HD), BF16),
            pltpu.VMEM((rows, 2 * HD), F32),
            pltpu.VMEM((rows, HD), F32),
            pltpu.VMEM((rows, HD), F32),
            pltpu.VMEM((rows, HD), F32),
            pltpu.VMEM((rows, HD), F32),
            pltpu.VMEM((group, 2 * tokens, HD), BF16),
            pltpu.VMEM((group, 2 * tokens, HD), BF16),
            pltpu.VMEM((group * HD, width), BF16),
            pltpu.SemaphoreType.DMA((6,)),
            pltpu.SemaphoreType.DMA((2,)),
            pltpu.SemaphoreType.DMA((group,)),
            pltpu.SemaphoreType.DMA((2, group)),
            pltpu.SemaphoreType.DMA((2, group)),
            pltpu.SemaphoreType.DMA((2, group)),
            pltpu.SemaphoreType.DMA((2, 2, half, 2)),
            pltpu.SemaphoreType.DMA((2, 2, half, 2)),
            pltpu.SemaphoreType.DMA((2, half, 2, 2)),
            pltpu.SemaphoreType.DMA((2, half, 2, 2)),
        ],
        compiler_params=pltpu.CompilerParams(
            collective_id=0, has_side_effects=True, vmem_limit_bytes=VMEM_LIMIT
        ),
        cost_estimate=pl.CostEstimate(
            flops=12 * rows * all_rows * HD,
            bytes_accessed=16 * all_rows * HD,
            transcendentals=rows * all_rows,
        ),
    )(
        queries,
        key_rows,
        values,
        query_tangent,
        key_tangent,
        value_tangent,
        out_weight,
        gate_vector,
        gate_tangent,
    )


def solution(mesh):
    rows = P(("dp", "seq", "head"), None)
    return jax.shard_map(
        functools.partial(local, seq_size=mesh.shape["seq"]),
        mesh=mesh,
        in_specs=(rows,) * 6 + (P(), P("dp"), P("dp")),
        out_specs=(rows, rows),
        check_vma=False,
    )
```

```python
import functools

import jax
import jax.numpy as jnp
from jax import lax
from jax.experimental import pallas as pl
from jax.experimental.pallas import tpu as pltpu
from jax.sharding import PartitionSpec as P

HD = 128
VMEM_LIMIT = 64 * 1024 * 1024
MESH = pl.DeviceIdType.MESH
SCALE = HD**-0.5
LOG2E = 1.4426950408889634
F32 = jnp.float32
BF16 = jnp.bfloat16
NEAR, FAR = 0, 1
LEFTWARD, RIGHTWARD = 0, 1


def kernel(
    nx,
    nz,
    q_hbm,
    k_hbm,
    v_hbm,
    qd_hbm,
    kd_hbm,
    vd_hbm,
    w_hbm,
    gate_hbm,
    gate_dot_hbm,
    out_ref,
    out_dot_ref,
    staged,
    gates,
    send_kv,
    send_q,
    land_kv,
    land_q,
    relay_kv,
    relay_q,
    kv,
    q_all,
    acc,
    acc_shaded,
    row_max,
    row_total,
    tilt_sum,
    out_send,
    out_land,
    weight,
    staged_sems,
    gate_sems,
    weight_sem,
    kv_sems,
    q_sems,
    relay_kv_sems,
    relay_q_sems,
    out_sems,
    ring_send_sems,
    ring_recv_sems,
    pair_send_sems,
    pair_recv_sems,
):
    tokens = q_hbm.shape[0]
    group = 2 * nx
    far_rows = nx * tokens
    half = nz // 2
    dp = lax.axis_index("dp")
    seq = lax.axis_index("seq")
    head_axis = lax.axis_index("head")
    z, x = seq // nx, seq % nx
    y, core = head_axis // 2, head_axis % 2

    def device(z_at, y_at, x_at, core_at):
        return (dp, z_at * nx + x_at, y_at * 2 + core_at)

    other_dp = (dp + 2) % 4
    other_y = ((y + (dp + 2) // 4) % 2, (y + (dp + 2) // 4 + 1) % 2)

    def along_y(way, dx):
        return (other_dp, z * nx + (x + dx) % nx, other_y[way] * 2 + core)

    def taker(j):
        return device(z, (y + j // nx) % 2, (x + j % nx) % nx, core)

    def giver(j):
        return device(z, (y + j // nx) % 2, (x + nx - j % nx) % nx, core)

    def head_of(j):
        return ((y + j // nx) % 2) * nx + (x + j % nx) % nx

    right = device((z + 1) % nz, y, x, core)
    left = device((z + nz - 1) % nz, y, x, core)
    sibling = device(z, y, x, 1 - core)

    staged_copies = [
        pltpu.make_async_copy(ref, staged.at[i], staged_sems.at[i])
        for i, ref in enumerate((k_hbm, kd_hbm, v_hbm, vd_hbm, q_hbm, qd_hbm))
    ]
    for copy in staged_copies:
        copy.start()
    weight_copies = [
        pltpu.make_async_copy(gate_hbm, gates.at[0, 0], gate_sems.at[0]),
        pltpu.make_async_copy(gate_dot_hbm, gates.at[1, 0], gate_sems.at[1]),
    ]
    for copy in weight_copies:
        copy.start()
    for j in range(group):
        rows = pl.ds(pl.multiple_of(head_of(j) * HD, HD), HD)
        copy = pltpu.make_async_copy(
            w_hbm.at[rows], weight.at[pl.ds(j * HD, HD)], weight_sem.at[j]
        )
        copy.start()
        weight_copies.append(copy)

    barrier = pltpu.get_barrier_semaphore()
    partners = [taker(j) for j in range(1, group)] + [sibling, right]
    partners += [along_y(way, dx) for way in (0, 1) for dx in range(nx)]
    if nz > 2:
        partners.append(left)
    for partner in partners:
        pl.semaphore_signal(barrier, inc=1, device_id=partner, device_id_type=MESH)

    for copy in staged_copies:
        copy.wait()
    for j in range(group):
        columns = pl.ds(pl.multiple_of(head_of(j) * HD, HD), HD)
        for part in (0, 1):
            send_kv[part, j] = jnp.concatenate(
                [staged[i, :, columns].astype(F32) for i in (2 * part, 2 * part + 1)], axis=0
            ).astype(BF16)
        send_q[j] = jnp.concatenate(
            [staged[i, :, columns].astype(F32) for i in (4, 5)], axis=0
        ).astype(BF16)

    pl.semaphore_wait(barrier, len(partners))

    def remote(src, dst, send_sem, recv_sem, to):
        return pltpu.make_async_remote_copy(
            src_ref=src,
            dst_ref=dst,
            send_sem=send_sem,
            recv_sem=recv_sem,
            device_id=to,
            device_id_type=MESH,
        )

    near_kv = [
        remote(
            send_kv.at[:, j], land_kv.at[:, j], kv_sems.at[0, 0, j], kv_sems.at[1, 0, j], taker(j)
        )
        for j in range(1, nx)
    ]
    near_q = [
        remote(send_q.at[j], land_q.at[j], q_sems.at[0, j], q_sems.at[1, j], taker(j))
        for j in range(1, nx)
    ]
    q_split = ((0, (nx + 1) // 2), ((nx + 1) // 2, nx))
    leg_q, leg_kv, far_q, far_kv = [], [], [], []
    for way in (0, 1):
        low, high = q_split[way]
        leg_kv.append(
            remote(
                send_kv.at[way, pl.ds(nx, nx)],
                relay_kv.at[way],
                relay_kv_sems.at[0, way],
                relay_kv_sems.at[1, way],
                along_y(way, 0),
            )
        )
        far_kv.append(
            [
                remote(
                    relay_kv.at[way, dx],
                    land_kv.at[way, nx + dx],
                    kv_sems.at[0, way, nx + dx],
                    kv_sems.at[1, way, nx + dx],
                    along_y(way, dx),
                )
                for dx in range(nx)
            ]
        )
        if high > low:
            leg_q.append(
                remote(
                    send_q.at[pl.ds(nx + low, high - low)],
                    relay_q.at[pl.ds(low, high - low)],
                    relay_q_sems.at[0, way],
                    relay_q_sems.at[1, way],
                    along_y(way, 0),
                )
            )
            far_q.append(
                [
                    remote(
                        relay_q.at[dx],
                        land_q.at[nx + dx],
                        q_sems.at[0, nx + dx],
                        q_sems.at[1, nx + dx],
                        along_y(way, dx),
                    )
                    for dx in range(low, high)
                ]
            )
    for copy in near_kv + leg_q + leg_kv + near_q:
        copy.start()

    def relay():
        for legs, onward in ((leg_q, far_q), (leg_kv, far_kv)):
            for leg, copies in zip(legs, onward):
                leg.wait_recv()
                for copy in copies:
                    copy.start()

    def slot(way, step):
        if step == 0:
            return half - 1, 0
        if step == half:
            return half - 1, 1
        return step - 1, way

    def steps_of(piece, way):
        return half if (piece == NEAR) == (way == RIGHTWARD) else half - 1

    ring_copies = {}
    pair_copies = {}
    for piece in (NEAR, FAR):
        for way in (LEFTWARD, RIGHTWARD):
            for step in range(1, steps_of(piece, way) + 1):
                for part in (0, 1):
                    from_p, from_sub = slot(way, step - 1)
                    to_p, to_sub = slot(way, step)
                    ring_copies[piece, way, step, part] = remote(
                        kv.at[piece, from_p, part, from_sub],
                        kv.at[piece, to_p, part, to_sub],
                        ring_send_sems.at[piece, way, step - 1, part],
                        ring_recv_sems.at[piece, way, step - 1, part],
                        right if way == RIGHTWARD else left,
                    )
        for p in range(half):
            for sub in (0, 1):
                for part in (0, 1):
                    pair_copies[piece, p, sub, part] = remote(
                        kv.at[piece, p, part, sub],
                        kv.at[piece, p, part, 2 + sub],
                        pair_send_sems.at[piece, p, sub, part],
                        pair_recv_sems.at[piece, p, sub, part],
                        sibling,
                    )

    def start_piece(piece):
        members = range(piece * nx, (piece + 1) * nx)
        for copy in near_kv if piece == NEAR else far_kv[0] + far_kv[1]:
            copy.wait_recv()
        for part in (0, 1):
            blocks = [(send_kv if j == 0 else land_kv)[part, j].astype(F32) for j in members]
            for side in (0, 1):
                at = side * tokens
                kv[piece, half - 1, part, 0, :, side * HD : (side + 1) * HD] = jnp.concatenate(
                    [block[at : at + tokens] for block in blocks], axis=0
                ).astype(BF16)
        for part in (0, 1):
            for way in (RIGHTWARD, LEFTWARD):
                if steps_of(piece, way) >= 1:
                    ring_copies[piece, way, 1, part].start()
        for part in (0, 1):
            pair_copies[piece, half - 1, 0, part].start()

    def pass_on(piece, step):
        for part in (0, 1):
            for way in (RIGHTWARD, LEFTWARD):
                if step <= steps_of(piece, way):
                    ring_copies[piece, way, step, part].wait_recv()
                    if step + 1 <= steps_of(piece, way):
                        ring_copies[piece, way, step + 1, part].start()
                    p, sub = slot(way, step)
                    pair_copies[piece, p, sub, part].start()

    def gather_queries():
        if gathered:
            return
        gathered.append(True)
        for copies in [near_q] + far_q:
            for copy in copies:
                copy.wait_recv()
        for side, at in ((0, tokens), (1, 0)):
            q_all[:, side * HD : (side + 1) * HD] = jnp.concatenate(
                [
                    (send_q if j == 0 else land_q)[j].astype(F32)[at : at + tokens]
                    for j in range(group)
                ],
                axis=0,
            ).astype(BF16)

    def absorb(piece, p, chunk):
        rows = pl.ds(pl.multiple_of(chunk * far_rows, 8), far_rows)
        query_rows = pl.ds(pl.multiple_of(chunk * far_rows, 16), far_rows)
        keys = kv[piece, p, 0].reshape(4 * far_rows, 2 * HD)
        vals = kv[piece, p, 1].reshape(4 * far_rows, 2 * HD)
        both = q_all[query_rows, :]
        transposed = (((1,), (1,)), ((), ()))
        scores = lax.dot_general(
            both[:, HD:], keys[:, :HD], transposed, preferred_element_type=F32
        ) * (SCALE * LOG2E)
        score_tangent = lax.dot_general(both, keys, transposed, preferred_element_type=F32)
        max_was = row_max[rows, :][:, :1]
        max_now = jnp.maximum(max_was, jnp.max(scores, axis=-1, keepdims=True))
        rescale = jnp.exp2(max_was - max_now)
        weights = jnp.exp2(scores - max_now).astype(BF16)
        wide = weights.astype(F32)
        shifted = wide * score_tangent
        shaded = shifted.astype(BF16)
        row_max[rows, :] = jnp.broadcast_to(max_now, (far_rows, HD))
        row_total[rows, :] = row_total[rows, :] * rescale + jnp.sum(wide, axis=-1, keepdims=True)
        tilt_sum[rows, :] = tilt_sum[rows, :] * rescale + jnp.sum(shifted, axis=-1, keepdims=True)
        acc[rows, :] = acc[rows, :] * rescale + jnp.dot(weights, vals, preferred_element_type=F32)
        acc_shaded[rows, :] = acc_shaded[rows, :] * rescale + jnp.dot(
            shaded, vals[:, :HD], preferred_element_type=F32
        )

    def absorb_all(piece, p):
        for sub in (0, 1):
            for part in (0, 1):
                pair_copies[piece, p, sub, part].wait_recv()

        def one(chunk, carry):
            absorb(piece, p, chunk)
            return carry

        lax.fori_loop(0, 2, one, 0)

    row_max[...] = jnp.full(row_max.shape, -1e30, F32)
    row_total[...] = jnp.zeros(row_total.shape, F32)
    tilt_sum[...] = jnp.zeros(tilt_sum.shape, F32)
    acc[...] = jnp.zeros(acc.shape, F32)
    acc_shaded[...] = jnp.zeros(acc_shaded.shape, F32)

    start_piece(NEAR)
    relay()
    order = [(NEAR, step) for step in range(1, min(half, 2) + 1)] + [(FAR, 0)]
    near_left = [(NEAR, step) for step in range(3, half + 1)]
    far_left = [(FAR, step) for step in range(1, half + 1)]
    while near_left or far_left:
        if near_left:
            order.append(near_left.pop(0))
        if far_left:
            order.append(far_left.pop(0))
    ready = []
    gathered = []
    for at, (piece, step) in enumerate(order):
        last = at == len(order) - 1
        if last:
            gather_queries()
            while ready:
                absorb_all(*ready.pop(0))
        if step == 0:
            start_piece(piece)
            continue
        pass_on(piece, step)
        if ready and not last:
            gather_queries()
            absorb_all(*ready.pop(0))
        ready.append((piece, step - 1))

    (piece, p), = ready
    for sub in (0, 1):
        for part in (0, 1):
            pair_copies[piece, p, sub, part].wait_recv()
    out_copies = [
        None
        if j == 0
        else remote(out_send.at[j], out_land.at[j], out_sems.at[0, j], out_sems.at[1, j], giver(j))
        for j in range(group)
    ]
    for chunk in (1, 0):
        absorb(piece, p, chunk)
        rows = slice(chunk * far_rows, (chunk + 1) * far_rows)
        inverse = 1.0 / row_total[rows, :]
        attended = acc[rows, :HD] * inverse
        tangent = acc[rows, HD:] + SCALE * acc_shaded[rows, :]
        attended_dot = tangent * inverse - (SCALE * tilt_sum[rows, :] * inverse) * attended
        for at in range(nx):
            j = chunk * nx + at
            own = slice(at * tokens, (at + 1) * tokens)
            block = jnp.concatenate([attended[own], attended_dot[own]], axis=0).astype(BF16)
            if j == 0:
                out_land[j] = block
            else:
                out_send[j] = block
                out_copies[j].start()

    for copy in weight_copies:
        copy.wait()
    for j in range(1, group):
        out_copies[j].wait_recv()
    everything = jnp.concatenate([out_land[j] for j in range(group)], axis=1)
    projected = jnp.dot(everything, weight[...], preferred_element_type=F32)
    primal, dot = projected[:tokens], projected[tokens:]
    gate, gate_dot = gates[0], gates[1]
    out_ref[...] = (gate * primal).astype(BF16)
    out_dot_ref[...] = (gate_dot * primal + gate * dot).astype(BF16)

    for j in range(1, group):
        out_copies[j].wait_send()
    for copies in [near_kv, near_q, leg_kv, leg_q] + far_kv + far_q:
        for copy in copies:
            copy.wait_send()
    for copy in ring_copies.values():
        copy.wait_send()
    for copy in pair_copies.values():
        copy.wait_send()


def local(
    queries,
    key_rows,
    values,
    query_tangent,
    key_tangent,
    value_tangent,
    out_weight,
    gate_vector,
    gate_tangent,
    *,
    seq_size,
):
    tokens = queries.shape[0]
    group = queries.shape[1] // HD
    nx = group // 2
    nz = seq_size // nx
    width = out_weight.shape[1]
    rows = group * tokens
    piece_rows = nx * tokens
    half = nz // 2
    vmem = pl.BlockSpec(memory_space=pltpu.VMEM)
    out_shape = jax.ShapeDtypeStruct((tokens, width), BF16)
    all_rows = rows * nz * 2
    return pl.pallas_call(
        functools.partial(kernel, nx, nz),
        out_shape=(out_shape, out_shape),
        in_specs=[pl.BlockSpec(memory_space=pl.ANY)] * 9,
        out_specs=(vmem, vmem),
        scratch_shapes=[
            pltpu.VMEM((6, tokens, group * HD), BF16),
            pltpu.VMEM((2, 1, width), F32),
            pltpu.VMEM((2, group, 2 * tokens, HD), BF16),
            pltpu.VMEM((group, 2 * tokens, HD), BF16),
            pltpu.VMEM((2, group, 2 * tokens, HD), BF16),
            pltpu.VMEM((group, 2 * tokens, HD), BF16),
            pltpu.VMEM((2, nx, 2 * tokens, HD), BF16),
            pltpu.VMEM((nx, 2 * tokens, HD), BF16),
            pltpu.VMEM((2, half, 2, 4, piece_rows, 2 * HD), BF16),
            pltpu.VMEM((rows, 2 * HD), BF16),
            pltpu.VMEM((rows, 2 * HD), F32),
            pltpu.VMEM((rows, HD), F32),
            pltpu.VMEM((rows, HD), F32),
            pltpu.VMEM((rows, HD), F32),
            pltpu.VMEM((rows, HD), F32),
            pltpu.VMEM((group, 2 * tokens, HD), BF16),
            pltpu.VMEM((group, 2 * tokens, HD), BF16),
            pltpu.VMEM((group * HD, width), BF16),
            pltpu.SemaphoreType.DMA((6,)),
            pltpu.SemaphoreType.DMA((2,)),
            pltpu.SemaphoreType.DMA((group,)),
            pltpu.SemaphoreType.DMA((2, 2, group)),
            pltpu.SemaphoreType.DMA((2, group)),
            pltpu.SemaphoreType.DMA((2, 2)),
            pltpu.SemaphoreType.DMA((2, 2)),
            pltpu.SemaphoreType.DMA((2, group)),
            pltpu.SemaphoreType.DMA((2, 2, half, 2)),
            pltpu.SemaphoreType.DMA((2, 2, half, 2)),
            pltpu.SemaphoreType.DMA((2, half, 2, 2)),
            pltpu.SemaphoreType.DMA((2, half, 2, 2)),
        ],
        compiler_params=pltpu.CompilerParams(
            collective_id=0, has_side_effects=True, vmem_limit_bytes=VMEM_LIMIT
        ),
        cost_estimate=pl.CostEstimate(
            flops=12 * rows * all_rows * HD,
            bytes_accessed=16 * all_rows * HD,
            transcendentals=rows * all_rows,
        ),
    )(
        queries,
        key_rows,
        values,
        query_tangent,
        key_tangent,
        value_tangent,
        out_weight,
        gate_vector,
        gate_tangent,
    )


def solution(mesh):
    rows = P(("dp", "seq", "head"), None)
    return jax.shard_map(
        functools.partial(local, seq_size=mesh.shape["seq"]),
        mesh=mesh,
        in_specs=(rows,) * 6 + (P(), P("dp"), P("dp")),
        out_specs=(rows, rows),
        check_vma=False,
    )
```

```python
import functools

import jax
import jax.numpy as jnp
from jax import lax
from jax.experimental import pallas as pl
from jax.experimental.pallas import tpu as pltpu
from jax.sharding import PartitionSpec as P

HD = 128
VMEM_LIMIT = 64 * 1024 * 1024
MESH = pl.DeviceIdType.MESH
SCALE = HD**-0.5
LOG2E = 1.4426950408889634
F32 = jnp.float32
BF16 = jnp.bfloat16
NEAR, FAR = 0, 1
LEFTWARD, RIGHTWARD = 0, 1


def kernel(
    nx,
    nz,
    q_hbm,
    k_hbm,
    v_hbm,
    qd_hbm,
    kd_hbm,
    vd_hbm,
    w_hbm,
    gate_hbm,
    gate_dot_hbm,
    out_ref,
    out_dot_ref,
    staged,
    gates,
    send_kv,
    send_q,
    land_kv,
    land_q,
    relay_kv,
    relay_q,
    kv,
    q_all,
    acc,
    acc_shaded,
    row_max,
    row_total,
    tilt_sum,
    out_send,
    out_land,
    weight,
    staged_sems,
    gate_sems,
    weight_sem,
    kv_sems,
    q_sems,
    relay_kv_sems,
    relay_q_sems,
    out_sems,
    ring_send_sems,
    ring_recv_sems,
    pair_send_sems,
    pair_recv_sems,
):
    tokens = q_hbm.shape[0]
    group = 2 * nx
    far_rows = nx * tokens
    half = nz // 2
    dp = lax.axis_index("dp")
    seq = lax.axis_index("seq")
    head_axis = lax.axis_index("head")
    z, x = seq // nx, seq % nx
    y, core = head_axis // 2, head_axis % 2

    def device(z_at, y_at, x_at, core_at):
        return (dp, z_at * nx + x_at, y_at * 2 + core_at)

    other_dp = (dp + 2) % 4
    other_y = ((y + (dp + 2) // 4) % 2, (y + (dp + 2) // 4 + 1) % 2)

    def along_y(way, dx):
        return (other_dp, z * nx + (x + dx) % nx, other_y[way] * 2 + core)

    def taker(j):
        return device(z, (y + j // nx) % 2, (x + j % nx) % nx, core)

    def giver(j):
        return device(z, (y + j // nx) % 2, (x + nx - j % nx) % nx, core)

    def head_of(j):
        return ((y + j // nx) % 2) * nx + (x + j % nx) % nx

    right = device((z + 1) % nz, y, x, core)
    left = device((z + nz - 1) % nz, y, x, core)
    sibling = device(z, y, x, 1 - core)

    staged_copies = [
        pltpu.make_async_copy(ref, staged.at[i], staged_sems.at[i])
        for i, ref in enumerate((k_hbm, kd_hbm, v_hbm, vd_hbm, q_hbm, qd_hbm))
    ]
    for copy in staged_copies:
        copy.start()
    weight_copies = [
        pltpu.make_async_copy(gate_hbm, gates.at[0, 0], gate_sems.at[0]),
        pltpu.make_async_copy(gate_dot_hbm, gates.at[1, 0], gate_sems.at[1]),
    ]
    for copy in weight_copies:
        copy.start()
    for j in range(group):
        rows = pl.ds(pl.multiple_of(head_of(j) * HD, HD), HD)
        copy = pltpu.make_async_copy(
            w_hbm.at[rows], weight.at[pl.ds(j * HD, HD)], weight_sem.at[j]
        )
        copy.start()
        weight_copies.append(copy)

    barrier = pltpu.get_barrier_semaphore()
    partners = [taker(j) for j in range(1, group)] + [sibling, right]
    partners += [along_y(way, dx) for way in (0, 1) for dx in range(nx)]
    if nz > 2:
        partners.append(left)
    for partner in partners:
        pl.semaphore_signal(barrier, inc=1, device_id=partner, device_id_type=MESH)

    for copy in staged_copies:
        copy.wait()
    for j in range(group):
        columns = pl.ds(pl.multiple_of(head_of(j) * HD, HD), HD)
        for part in (0, 1):
            send_kv[part, j] = jnp.concatenate(
                [staged[i, :, columns].astype(F32) for i in (2 * part, 2 * part + 1)], axis=0
            ).astype(BF16)
        send_q[j] = jnp.concatenate(
            [staged[i, :, columns].astype(F32) for i in (4, 5)], axis=0
        ).astype(BF16)

    pl.semaphore_wait(barrier, len(partners))

    def remote(src, dst, send_sem, recv_sem, to):
        return pltpu.make_async_remote_copy(
            src_ref=src,
            dst_ref=dst,
            send_sem=send_sem,
            recv_sem=recv_sem,
            device_id=to,
            device_id_type=MESH,
        )

    near_kv = [
        remote(
            send_kv.at[:, j], land_kv.at[:, j], kv_sems.at[0, 0, j], kv_sems.at[1, 0, j], taker(j)
        )
        for j in range(1, nx)
    ]
    near_q = [
        remote(send_q.at[j], land_q.at[j], q_sems.at[0, j], q_sems.at[1, j], taker(j))
        for j in range(1, nx)
    ]
    q_split = ((0, (nx + 1) // 2), ((nx + 1) // 2, nx))
    leg_q, leg_kv, far_q, far_kv = [], [], [], []
    for way in (0, 1):
        low, high = q_split[way]
        leg_kv.append(
            remote(
                send_kv.at[way, pl.ds(nx, nx)],
                relay_kv.at[way],
                relay_kv_sems.at[0, way],
                relay_kv_sems.at[1, way],
                along_y(way, 0),
            )
        )
        far_kv.append(
            [
                remote(
                    relay_kv.at[way, dx],
                    land_kv.at[way, nx + dx],
                    kv_sems.at[0, way, nx + dx],
                    kv_sems.at[1, way, nx + dx],
                    along_y(way, dx),
                )
                for dx in range(nx)
            ]
        )
        if high > low:
            leg_q.append(
                remote(
                    send_q.at[pl.ds(nx + low, high - low)],
                    relay_q.at[pl.ds(low, high - low)],
                    relay_q_sems.at[0, way],
                    relay_q_sems.at[1, way],
                    along_y(way, 0),
                )
            )
            far_q.append(
                [
                    remote(
                        relay_q.at[dx],
                        land_q.at[nx + dx],
                        q_sems.at[0, nx + dx],
                        q_sems.at[1, nx + dx],
                        along_y(way, dx),
                    )
                    for dx in range(low, high)
                ]
            )
    for copy in near_kv + leg_q + leg_kv + near_q:
        copy.start()

    def relay():
        for legs, onward in ((leg_q, far_q), (leg_kv, far_kv)):
            for leg, copies in zip(legs, onward):
                leg.wait_recv()
                for copy in copies:
                    copy.start()

    def slot(way, step):
        if step == 0:
            return half - 1, 0
        if step == half:
            return half - 1, 1
        return step - 1, way

    def steps_of(piece, way):
        return half if (piece == NEAR) == (way == RIGHTWARD) else half - 1

    ring_copies = {}
    for piece in (NEAR, FAR):
        for way in (LEFTWARD, RIGHTWARD):
            for step in range(1, steps_of(piece, way) + 1):
                for part in (0, 1):
                    from_p, from_sub = slot(way, step - 1)
                    to_p, to_sub = slot(way, step)
                    ring_copies[piece, way, step, part] = remote(
                        kv.at[piece, from_p, part, from_sub],
                        kv.at[piece, to_p, part, to_sub],
                        ring_send_sems.at[piece, way, step - 1, part],
                        ring_recv_sems.at[piece, way, step - 1, part],
                        right if way == RIGHTWARD else left,
                    )

    def pair_copy(piece, p, sub, part):
        return remote(
            kv.at[piece, p, part, sub],
            kv.at[piece, p, part, 2 + sub],
            pair_send_sems.at[piece, p, sub, part],
            pair_recv_sems.at[piece, p, sub, part],
            sibling,
        )

    def start_piece(piece):
        members = range(piece * nx, (piece + 1) * nx)
        for copy in near_kv if piece == NEAR else far_kv[0] + far_kv[1]:
            copy.wait_recv()
        for part in (0, 1):
            blocks = [(send_kv if j == 0 else land_kv)[part, j].astype(F32) for j in members]
            for side in (0, 1):
                at = side * tokens
                kv[piece, half - 1, part, 0, :, side * HD : (side + 1) * HD] = jnp.concatenate(
                    [block[at : at + tokens] for block in blocks], axis=0
                ).astype(BF16)
        for part in (0, 1):
            for way in (RIGHTWARD, LEFTWARD):
                if steps_of(piece, way) >= 1:
                    ring_copies[piece, way, 1, part].start()
        for part in (0, 1):
            pair_copy(piece, half - 1, 0, part).start()

    def pass_on(piece, step):
        for part in (0, 1):
            for way in (RIGHTWARD, LEFTWARD) if piece == NEAR else (LEFTWARD, RIGHTWARD):
                if step <= steps_of(piece, way):
                    ring_copies[piece, way, step, part].wait_recv()
                    if step + 1 <= steps_of(piece, way):
                        ring_copies[piece, way, step + 1, part].start()
                    p, sub = slot(way, step)
                    pair_copy(piece, p, sub, part).start()

    def gather_queries():
        for copies in [near_q] + far_q:
            for copy in copies:
                copy.wait_recv()
        for side, at in ((0, tokens), (1, 0)):
            q_all[:, side * HD : (side + 1) * HD] = jnp.concatenate(
                [
                    (send_q if j == 0 else land_q)[j].astype(F32)[at : at + tokens]
                    for j in range(group)
                ],
                axis=0,
            ).astype(BF16)

    def absorb(piece, p):
        keys = kv[piece, p, 0].reshape(4 * far_rows, 2 * HD)
        vals = kv[piece, p, 1].reshape(4 * far_rows, 2 * HD)
        both = q_all[...]
        transposed = (((1,), (1,)), ((), ()))
        scores = lax.dot_general(
            both[:, HD:], keys[:, :HD], transposed, preferred_element_type=F32
        ) * (SCALE * LOG2E)
        score_tangent = lax.dot_general(both, keys, transposed, preferred_element_type=F32)
        max_was = row_max[...][:, :1]
        max_now = jnp.maximum(max_was, jnp.max(scores, axis=-1, keepdims=True))
        rescale = jnp.exp2(max_was - max_now)
        weights = jnp.exp2(scores - max_now).astype(BF16)
        wide = weights.astype(F32)
        shifted = wide * score_tangent
        shaded = shifted.astype(BF16)
        row_max[...] = jnp.broadcast_to(max_now, row_max.shape)
        row_total[...] = row_total[...] * rescale + jnp.sum(wide, axis=-1, keepdims=True)
        tilt_sum[...] = tilt_sum[...] * rescale + jnp.sum(shifted, axis=-1, keepdims=True)
        acc[...] = acc[...] * rescale + jnp.dot(weights, vals, preferred_element_type=F32)
        acc_shaded[...] = acc_shaded[...] * rescale + jnp.dot(
            shaded, vals[:, :HD], preferred_element_type=F32
        )

    row_max[...] = jnp.full(row_max.shape, -1e30, F32)
    row_total[...] = jnp.zeros(row_total.shape, F32)
    tilt_sum[...] = jnp.zeros(tilt_sum.shape, F32)
    acc[...] = jnp.zeros(acc.shape, F32)
    acc_shaded[...] = jnp.zeros(acc_shaded.shape, F32)

    start_piece(NEAR)
    relay()

    before = {at: [] for at in range(2 * half)}
    for step in range(1, min(half, 2) + 1):
        before[0].append((NEAR, step))
    at = 1
    for step in range(1, half + 1):
        if step + 2 <= half:
            before[at].append((NEAR, step + 2))
            at += 1
        before[2 * half - 1 if step == half else at].append((FAR, step))
        at += 1

    def block(at, carry):
        for now, arrivals in before.items():
            if not arrivals:
                continue

            @pl.when(at == now)
            def _(now=now, arrivals=arrivals):
                for piece, step in arrivals:
                    pass_on(piece, step)
                if now == 0:
                    start_piece(FAR)
                    gather_queries()

        piece, p = at // half, at % half
        for sub in (0, 1):
            for part in (0, 1):
                pair_copy(piece, p, sub, part).wait_recv()
        absorb(piece, p)
        return carry

    lax.fori_loop(0, 2 * half, block, 0)

    out_copies = [
        None
        if j == 0
        else remote(out_send.at[j], out_land.at[j], out_sems.at[0, j], out_sems.at[1, j], giver(j))
        for j in range(group)
    ]
    for chunk in (1, 0):
        rows = slice(chunk * far_rows, (chunk + 1) * far_rows)
        inverse = 1.0 / row_total[rows, :]
        attended = acc[rows, :HD] * inverse
        tangent = acc[rows, HD:] + SCALE * acc_shaded[rows, :]
        attended_dot = tangent * inverse - (SCALE * tilt_sum[rows, :] * inverse) * attended
        for at in range(nx):
            j = chunk * nx + at
            own = slice(at * tokens, (at + 1) * tokens)
            block = jnp.concatenate([attended[own], attended_dot[own]], axis=0).astype(BF16)
            if j == 0:
                out_land[j] = block
            else:
                out_send[j] = block
                out_copies[j].start()

    for copy in weight_copies:
        copy.wait()
    for j in range(1, group):
        out_copies[j].wait_recv()
    everything = jnp.concatenate([out_land[j] for j in range(group)], axis=1)
    projected = jnp.dot(everything, weight[...], preferred_element_type=F32)
    primal, dot = projected[:tokens], projected[tokens:]
    gate, gate_dot = gates[0], gates[1]
    out_ref[...] = (gate * primal).astype(BF16)
    out_dot_ref[...] = (gate_dot * primal + gate * dot).astype(BF16)

    for j in range(1, group):
        out_copies[j].wait_send()
    for copies in [near_kv, near_q, leg_kv, leg_q] + far_kv + far_q:
        for copy in copies:
            copy.wait_send()
    for copy in ring_copies.values():
        copy.wait_send()
    for piece in (NEAR, FAR):
        for p in range(half):
            for sub in (0, 1):
                for part in (0, 1):
                    pair_copy(piece, p, sub, part).wait_send()


def local(
    queries,
    key_rows,
    values,
    query_tangent,
    key_tangent,
    value_tangent,
    out_weight,
    gate_vector,
    gate_tangent,
    *,
    seq_size,
):
    tokens = queries.shape[0]
    group = queries.shape[1] // HD
    nx = group // 2
    nz = seq_size // nx
    width = out_weight.shape[1]
    rows = group * tokens
    piece_rows = nx * tokens
    half = nz // 2
    vmem = pl.BlockSpec(memory_space=pltpu.VMEM)
    out_shape = jax.ShapeDtypeStruct((tokens, width), BF16)
    all_rows = rows * nz * 2
    return pl.pallas_call(
        functools.partial(kernel, nx, nz),
        out_shape=(out_shape, out_shape),
        in_specs=[pl.BlockSpec(memory_space=pl.ANY)] * 9,
        out_specs=(vmem, vmem),
        scratch_shapes=[
            pltpu.VMEM((6, tokens, group * HD), BF16),
            pltpu.VMEM((2, 1, width), F32),
            pltpu.VMEM((2, group, 2 * tokens, HD), BF16),
            pltpu.VMEM((group, 2 * tokens, HD), BF16),
            pltpu.VMEM((2, group, 2 * tokens, HD), BF16),
            pltpu.VMEM((group, 2 * tokens, HD), BF16),
            pltpu.VMEM((2, nx, 2 * tokens, HD), BF16),
            pltpu.VMEM((nx, 2 * tokens, HD), BF16),
            pltpu.VMEM((2, half, 2, 4, piece_rows, 2 * HD), BF16),
            pltpu.VMEM((rows, 2 * HD), BF16),
            pltpu.VMEM((rows, 2 * HD), F32),
            pltpu.VMEM((rows, HD), F32),
            pltpu.VMEM((rows, HD), F32),
            pltpu.VMEM((rows, HD), F32),
            pltpu.VMEM((rows, HD), F32),
            pltpu.VMEM((group, 2 * tokens, HD), BF16),
            pltpu.VMEM((group, 2 * tokens, HD), BF16),
            pltpu.VMEM((group * HD, width), BF16),
            pltpu.SemaphoreType.DMA((6,)),
            pltpu.SemaphoreType.DMA((2,)),
            pltpu.SemaphoreType.DMA((group,)),
            pltpu.SemaphoreType.DMA((2, 2, group)),
            pltpu.SemaphoreType.DMA((2, group)),
            pltpu.SemaphoreType.DMA((2, 2)),
            pltpu.SemaphoreType.DMA((2, 2)),
            pltpu.SemaphoreType.DMA((2, group)),
            pltpu.SemaphoreType.DMA((2, 2, half, 2)),
            pltpu.SemaphoreType.DMA((2, 2, half, 2)),
            pltpu.SemaphoreType.DMA((2, half, 2, 2)),
            pltpu.SemaphoreType.DMA((2, half, 2, 2)),
        ],
        compiler_params=pltpu.CompilerParams(
            collective_id=0, has_side_effects=True, vmem_limit_bytes=VMEM_LIMIT
        ),
        cost_estimate=pl.CostEstimate(
            flops=12 * rows * all_rows * HD,
            bytes_accessed=16 * all_rows * HD,
            transcendentals=rows * all_rows,
        ),
    )(
        queries,
        key_rows,
        values,
        query_tangent,
        key_tangent,
        value_tangent,
        out_weight,
        gate_vector,
        gate_tangent,
    )


def solution(mesh):
    rows = P(("dp", "seq", "head"), None)
    return jax.shard_map(
        functools.partial(local, seq_size=mesh.shape["seq"]),
        mesh=mesh,
        in_specs=(rows,) * 6 + (P(), P("dp"), P("dp")),
        out_specs=(rows, rows),
        check_vma=False,
    )
```

```python
import functools

import jax
import jax.numpy as jnp
from jax import lax
from jax.experimental import pallas as pl
from jax.experimental.pallas import tpu as pltpu
from jax.sharding import PartitionSpec as P

HD = 128
VMEM_LIMIT = 64 * 1024 * 1024
MESH = pl.DeviceIdType.MESH
SCALE = HD**-0.5
F32 = jnp.float32
BF16 = jnp.bfloat16
NEAR, FAR = 0, 1
LEFTWARD, RIGHTWARD = 0, 1


def kernel(
    nx,
    nz,
    q_hbm,
    k_hbm,
    v_hbm,
    qd_hbm,
    kd_hbm,
    vd_hbm,
    w_hbm,
    out_ref,
    staged,
    send_kv,
    send_q,
    land_kv,
    land_q,
    relay_kv,
    relay_q,
    kv,
    q_all,
    acc,
    acc_shaded,
    row_max,
    row_total,
    tilt_sum,
    out_send,
    out_land,
    weight,
    staged_sems,
    weight_sem,
    kv_sems,
    q_sems,
    relay_kv_sems,
    relay_q_sems,
    out_sems,
    ring_send_sems,
    ring_recv_sems,
    pair_send_sems,
    pair_recv_sems,
):
    tokens = q_hbm.shape[0]
    group = 2 * nx
    far_rows = nx * tokens
    half = nz // 2
    dp = lax.axis_index("dp")
    seq = lax.axis_index("seq")
    head_axis = lax.axis_index("head")
    z, x = seq // nx, seq % nx
    y, core = head_axis // 2, head_axis % 2

    def device(z_at, y_at, x_at, core_at):
        return (dp, z_at * nx + x_at, y_at * 2 + core_at)

    other_dp = (dp + 2) % 4
    other_y = ((y + (dp + 2) // 4) % 2, (y + (dp + 2) // 4 + 1) % 2)

    def along_y(way, dx):
        return (other_dp, z * nx + (x + dx) % nx, other_y[way] * 2 + core)

    def taker(j):
        return device(z, (y + j // nx) % 2, (x + j % nx) % nx, core)

    def giver(j):
        return device(z, (y + j // nx) % 2, (x + nx - j % nx) % nx, core)

    def head_of(j):
        return ((y + j // nx) % 2) * nx + (x + j % nx) % nx

    right = device((z + 1) % nz, y, x, core)
    left = device((z + nz - 1) % nz, y, x, core)
    sibling = device(z, y, x, 1 - core)

    staged_copies = [
        pltpu.make_async_copy(ref, staged.at[i], staged_sems.at[i])
        for i, ref in enumerate((k_hbm, kd_hbm, v_hbm, vd_hbm, q_hbm, qd_hbm))
    ]
    for copy in staged_copies:
        copy.start()
    weight_copies = []
    for j in range(group):
        rows = pl.ds(pl.multiple_of(head_of(j) * HD, HD), HD)
        copy = pltpu.make_async_copy(
            w_hbm.at[rows], weight.at[pl.ds(j * HD, HD)], weight_sem.at[j]
        )
        copy.start()
        weight_copies.append(copy)

    barrier = pltpu.get_barrier_semaphore()
    partners = [taker(j) for j in range(1, group)] + [sibling, right]
    partners += [along_y(way, dx) for way in (0, 1) for dx in range(nx)]
    if nz > 2:
        partners.append(left)
    for partner in partners:
        pl.semaphore_signal(barrier, inc=1, device_id=partner, device_id_type=MESH)

    for copy in staged_copies:
        copy.wait()
    for j in range(group):
        columns = pl.ds(pl.multiple_of(head_of(j) * HD, HD), HD)
        for part in (0, 1):
            send_kv[part, j] = jnp.concatenate(
                [staged[i, :, columns].astype(F32) for i in (2 * part, 2 * part + 1)], axis=0
            ).astype(BF16)
        send_q[j] = jnp.concatenate(
            [staged[i, :, columns].astype(F32) for i in (4, 5)], axis=0
        ).astype(BF16)

    pl.semaphore_wait(barrier, len(partners))

    def remote(src, dst, send_sem, recv_sem, to):
        return pltpu.make_async_remote_copy(
            src_ref=src,
            dst_ref=dst,
            send_sem=send_sem,
            recv_sem=recv_sem,
            device_id=to,
            device_id_type=MESH,
        )

    near_kv = [
        remote(
            send_kv.at[:, j], land_kv.at[:, j], kv_sems.at[0, 0, j], kv_sems.at[1, 0, j], taker(j)
        )
        for j in range(1, nx)
    ]
    near_q = [
        remote(send_q.at[j], land_q.at[j], q_sems.at[0, j], q_sems.at[1, j], taker(j))
        for j in range(1, nx)
    ]
    q_split = ((0, (nx + 1) // 2), ((nx + 1) // 2, nx))
    leg_q, leg_kv, far_q, far_kv = [], [], [], []
    for way in (0, 1):
        low, high = q_split[way]
        leg_kv.append(
            remote(
                send_kv.at[way, pl.ds(nx, nx)],
                relay_kv.at[way],
                relay_kv_sems.at[0, way],
                relay_kv_sems.at[1, way],
                along_y(way, 0),
            )
        )
        far_kv.append(
            [
                remote(
                    relay_kv.at[way, dx],
                    land_kv.at[way, nx + dx],
                    kv_sems.at[0, way, nx + dx],
                    kv_sems.at[1, way, nx + dx],
                    along_y(way, dx),
                )
                for dx in range(nx)
            ]
        )
        if high > low:
            leg_q.append(
                remote(
                    send_q.at[pl.ds(nx + low, high - low)],
                    relay_q.at[pl.ds(low, high - low)],
                    relay_q_sems.at[0, way],
                    relay_q_sems.at[1, way],
                    along_y(way, 0),
                )
            )
            far_q.append(
                [
                    remote(
                        relay_q.at[dx],
                        land_q.at[nx + dx],
                        q_sems.at[0, nx + dx],
                        q_sems.at[1, nx + dx],
                        along_y(way, dx),
                    )
                    for dx in range(low, high)
                ]
            )
    for copy in near_kv + leg_q + leg_kv + near_q:
        copy.start()

    def relay():
        for legs, onward in ((leg_q, far_q), (leg_kv, far_kv)):
            for leg, copies in zip(legs, onward):
                leg.wait_recv()
                for copy in copies:
                    copy.start()

    def slot(way, step):
        if step == 0:
            return half - 1, 0
        if step == half:
            return half - 1, 1
        return step - 1, way

    def steps_of(piece, way):
        return half if (piece == NEAR) == (way == RIGHTWARD) else half - 1

    ring_copies = {}
    part_rows = (pl.ds(0, far_rows // 2), pl.ds(far_rows // 2, far_rows // 2))
    for piece in (NEAR, FAR):
        for way in (LEFTWARD, RIGHTWARD):
            for step in range(1, steps_of(piece, way) + 1):
                for part in range(4):
                    from_p, from_sub = slot(way, step - 1)
                    to_p, to_sub = slot(way, step)
                    ring_copies[piece, way, step, part] = remote(
                        kv.at[piece, from_p, part // 2, from_sub, part_rows[part % 2]],
                        kv.at[piece, to_p, part // 2, to_sub, part_rows[part % 2]],
                        ring_send_sems.at[piece, way, step - 1, part],
                        ring_recv_sems.at[piece, way, step - 1, part],
                        right if way == RIGHTWARD else left,
                    )

    def pair_copy(piece, p, sub):
        return remote(
            kv.at[piece, p, :, sub],
            kv.at[piece, p, :, 2 + sub],
            pair_send_sems.at[piece, p, sub],
            pair_recv_sems.at[piece, p, sub],
            sibling,
        )

    def start_piece(piece):
        members = range(piece * nx, (piece + 1) * nx)
        for copy in near_kv if piece == NEAR else far_kv[0] + far_kv[1]:
            copy.wait_recv()
        for part in (0, 1):
            blocks = [(send_kv if j == 0 else land_kv)[part, j].astype(F32) for j in members]
            for side in (0, 1):
                at = side * tokens
                kv[piece, half - 1, part, 0, :, side * HD : (side + 1) * HD] = jnp.concatenate(
                    [block[at : at + tokens] for block in blocks], axis=0
                ).astype(BF16)
        for part in range(4):
            for way in (RIGHTWARD, LEFTWARD):
                if steps_of(piece, way) >= 1:
                    ring_copies[piece, way, 1, part].start()
        pair_copy(piece, half - 1, 0).start()

    def pass_on(piece, step):
        for part in range(4):
            for way in (RIGHTWARD, LEFTWARD) if piece == NEAR else (LEFTWARD, RIGHTWARD):
                if step <= steps_of(piece, way):
                    ring_copies[piece, way, step, part].wait_recv()
                    if step + 1 <= steps_of(piece, way):
                        ring_copies[piece, way, step + 1, part].start()
                    if part == 3:
                        pair_copy(piece, *slot(way, step)).start()

    def gather_queries():
        for copies in [near_q] + far_q:
            for copy in copies:
                copy.wait_recv()
        for side, at in ((0, tokens), (1, 0)):
            q_all[:, side * HD : (side + 1) * HD] = jnp.concatenate(
                [
                    (send_q if j == 0 else land_q)[j].astype(F32)[at : at + tokens]
                    for j in range(group)
                ],
                axis=0,
            ).astype(BF16)

    def by_lane(block):
        total = block[:, :HD]
        for at in range(HD, block.shape[1], HD):
            total = total + block[:, at : at + HD]
        return total

    def absorb(piece, p):
        keys = kv[piece, p, 0].reshape(4 * far_rows, 2 * HD)
        vals = kv[piece, p, 1].reshape(4 * far_rows, 2 * HD)
        both = q_all[...]
        transposed = (((1,), (1,)), ((), ()))
        scores = lax.dot_general(
            both[:, HD:], keys[:, :HD], transposed, preferred_element_type=F32
        ) * SCALE
        score_tangent = lax.dot_general(both, keys, transposed, preferred_element_type=F32)
        max_was = row_max[...][:, :1]
        max_now = jnp.maximum(max_was, jnp.max(scores, axis=-1, keepdims=True))
        rescale = jnp.exp(max_was - max_now)
        weights = jnp.exp(scores - max_now).astype(BF16)
        wide = weights.astype(F32)
        shifted = wide * score_tangent
        shaded = shifted.astype(BF16)
        row_max[...] = jnp.broadcast_to(max_now, row_max.shape)
        row_total[...] = row_total[...] * rescale + by_lane(wide)
        tilt_sum[...] = tilt_sum[...] * rescale + by_lane(shifted)
        acc[...] = acc[...] * rescale + jnp.dot(weights, vals, preferred_element_type=F32)
        acc_shaded[...] = acc_shaded[...] * rescale + jnp.dot(
            shaded, vals[:, :HD], preferred_element_type=F32
        )

    row_max[...] = jnp.full(row_max.shape, -1e30, F32)
    row_total[...] = jnp.zeros(row_total.shape, F32)
    tilt_sum[...] = jnp.zeros(tilt_sum.shape, F32)
    acc[...] = jnp.zeros(acc.shape, F32)
    acc_shaded[...] = jnp.zeros(acc_shaded.shape, F32)

    start_piece(NEAR)
    relay()

    before = {at: [] for at in range(2 * half)}
    for step in range(1, min(half, 2) + 1):
        before[0].append((NEAR, step))
    at = 1
    for step in range(1, half + 1):
        if step + 2 <= half:
            before[at].append((NEAR, step + 2))
            at += 1
        before[2 * half - 1 if step == half else at].append((FAR, step))
        at += 1

    def block(at, carry):
        for now, arrivals in before.items():
            if not arrivals:
                continue

            @pl.when(at == now)
            def _(now=now, arrivals=arrivals):
                for piece, step in arrivals:
                    pass_on(piece, step)
                if now == 0:
                    start_piece(FAR)
                    gather_queries()

        piece, p = at // half, at % half
        for sub in (0, 1):
            pair_copy(piece, p, sub).wait_recv()
        absorb(piece, p)
        return carry

    lax.fori_loop(0, 2 * half, block, 0)

    out_copies = [
        None
        if j == 0
        else remote(out_send.at[j], out_land.at[j], out_sems.at[0, j], out_sems.at[1, j], giver(j))
        for j in range(group)
    ]
    for chunk in (1, 0):
        rows = slice(chunk * far_rows, (chunk + 1) * far_rows)
        inverse = 1.0 / jnp.sum(row_total[rows, :], axis=-1, keepdims=True)
        tilt = SCALE * jnp.sum(tilt_sum[rows, :], axis=-1, keepdims=True) * inverse
        attended = acc[rows, :HD] * inverse
        tangent = acc[rows, HD:] + SCALE * acc_shaded[rows, :]
        attended_dot = tangent * inverse - tilt * attended
        for at in range(nx):
            j = chunk * nx + at
            own = slice(at * tokens, (at + 1) * tokens)
            block = jnp.concatenate([attended[own], attended_dot[own]], axis=0).astype(BF16)
            if j == 0:
                out_land[j] = block
            else:
                out_send[j] = block
                out_copies[j].start()

    for copy in weight_copies:
        copy.wait()
    for j in range(1, group):
        out_copies[j].wait_recv()
    everything = jnp.concatenate([out_land[j] for j in range(group)], axis=1)
    out_ref[...] = jnp.dot(everything, weight[...], preferred_element_type=F32)

    for j in range(1, group):
        out_copies[j].wait_send()
    for copies in [near_kv, near_q, leg_kv, leg_q] + far_kv + far_q:
        for copy in copies:
            copy.wait_send()
    for copy in ring_copies.values():
        copy.wait_send()
    for piece in (NEAR, FAR):
        for p in range(half):
            for sub in (0, 1):
                pair_copy(piece, p, sub).wait_send()


def local(
    queries,
    key_rows,
    values,
    query_tangent,
    key_tangent,
    value_tangent,
    out_weight,
    gate_vector,
    gate_tangent,
    *,
    seq_size,
):
    tokens = queries.shape[0]
    group = queries.shape[1] // HD
    nx = group // 2
    nz = seq_size // nx
    width = out_weight.shape[1]
    rows = group * tokens
    piece_rows = nx * tokens
    half = nz // 2
    vmem = pl.BlockSpec(memory_space=pltpu.VMEM)
    all_rows = rows * nz * 2
    projected = pl.pallas_call(
        functools.partial(kernel, nx, nz),
        out_shape=jax.ShapeDtypeStruct((2 * tokens, width), F32),
        in_specs=[pl.BlockSpec(memory_space=pl.ANY)] * 7,
        out_specs=vmem,
        scratch_shapes=[
            pltpu.VMEM((6, tokens, group * HD), BF16),
            pltpu.VMEM((2, group, 2 * tokens, HD), BF16),
            pltpu.VMEM((group, 2 * tokens, HD), BF16),
            pltpu.VMEM((2, group, 2 * tokens, HD), BF16),
            pltpu.VMEM((group, 2 * tokens, HD), BF16),
            pltpu.VMEM((2, nx, 2 * tokens, HD), BF16),
            pltpu.VMEM((nx, 2 * tokens, HD), BF16),
            pltpu.VMEM((2, half, 2, 4, piece_rows, 2 * HD), BF16),
            pltpu.VMEM((rows, 2 * HD), BF16),
            pltpu.VMEM((rows, 2 * HD), F32),
            pltpu.VMEM((rows, HD), F32),
            pltpu.VMEM((rows, HD), F32),
            pltpu.VMEM((rows, HD), F32),
            pltpu.VMEM((rows, HD), F32),
            pltpu.VMEM((group, 2 * tokens, HD), BF16),
            pltpu.VMEM((group, 2 * tokens, HD), BF16),
            pltpu.VMEM((group * HD, width), BF16),
            pltpu.SemaphoreType.DMA((6,)),
            pltpu.SemaphoreType.DMA((group,)),
            pltpu.SemaphoreType.DMA((2, 2, group)),
            pltpu.SemaphoreType.DMA((2, group)),
            pltpu.SemaphoreType.DMA((2, 2)),
            pltpu.SemaphoreType.DMA((2, 2)),
            pltpu.SemaphoreType.DMA((2, group)),
            pltpu.SemaphoreType.DMA((2, 2, half, 4)),
            pltpu.SemaphoreType.DMA((2, 2, half, 4)),
            pltpu.SemaphoreType.DMA((2, half, 2)),
            pltpu.SemaphoreType.DMA((2, half, 2)),
        ],
        compiler_params=pltpu.CompilerParams(
            collective_id=0, has_side_effects=True, vmem_limit_bytes=VMEM_LIMIT
        ),
        cost_estimate=pl.CostEstimate(
            flops=12 * rows * all_rows * HD,
            bytes_accessed=16 * all_rows * HD,
            transcendentals=rows * all_rows,
        ),
    )(
        queries,
        key_rows,
        values,
        query_tangent,
        key_tangent,
        value_tangent,
        out_weight,
    )
    primal, dot = projected[:tokens], projected[tokens:]
    block_out = (gate_vector * primal).astype(BF16)
    block_tangent = (gate_tangent * primal + gate_vector * dot).astype(BF16)
    return block_out, block_tangent


def solution(mesh):
    rows = P(("dp", "seq", "head"), None)
    return jax.shard_map(
        functools.partial(local, seq_size=mesh.shape["seq"]),
        mesh=mesh,
        in_specs=(rows,) * 6 + (P(), P("dp"), P("dp")),
        out_specs=(rows, rows),
        check_vma=False,
    )
```

```python
import functools

import jax
import jax.numpy as jnp
from jax import lax
from jax.experimental import pallas as pl
from jax.experimental.pallas import tpu as pltpu
from jax.sharding import PartitionSpec as P

HD = 128
VMEM_LIMIT = 64 * 1024 * 1024
MESH = pl.DeviceIdType.MESH
SCALE = HD**-0.5
F32 = jnp.float32
BF16 = jnp.bfloat16
NEAR, FAR = 0, 1
LEFTWARD, RIGHTWARD = 0, 1


def kernel(
    nx,
    nz,
    q_hbm,
    k_hbm,
    v_hbm,
    qd_hbm,
    kd_hbm,
    vd_hbm,
    w_hbm,
    out_ref,
    staged,
    send_kv,
    send_q,
    land_kv,
    land_q,
    relay_kv,
    relay_q,
    kv,
    q_all,
    acc,
    acc_shaded,
    row_max,
    row_total,
    tilt_sum,
    merge_send,
    merge_land,
    out_send,
    out_land,
    weight,
    staged_sems,
    weight_sem,
    kv_sems,
    q_sems,
    relay_kv_sems,
    relay_q_sems,
    out_sems,
    ring_send_sems,
    ring_recv_sems,
    pair_sems,
):
    tokens = q_hbm.shape[0]
    group = 2 * nx
    far_rows = nx * tokens
    rows_own = 2 * far_rows
    half = nz // 2
    dp = lax.axis_index("dp")
    seq = lax.axis_index("seq")
    head_axis = lax.axis_index("head")
    z, x = seq // nx, seq % nx
    y, core = head_axis // 2, head_axis % 2

    def device(z_at, y_at, x_at, core_at):
        return (dp, z_at * nx + x_at, y_at * 2 + core_at)

    other_dp = (dp + 2) % 4
    other_y = ((y + (dp + 2) // 4) % 2, (y + (dp + 2) // 4 + 1) % 2)

    def along_y(way, dx):
        return (other_dp, z * nx + (x + dx) % nx, other_y[way] * 2 + core)

    def taker(j):
        return device(z, (y + j // nx) % 2, (x + j % nx) % nx, core)

    def giver(j):
        return device(z, (y + j // nx) % 2, (x + nx - j % nx) % nx, core)

    def head_of(j):
        return ((y + j // nx) % 2) * nx + (x + j % nx) % nx

    right = device((z + 1) % nz, y, x, core)
    left = device((z + nz - 1) % nz, y, x, core)
    sibling = device(z, y, x, 1 - core)

    staged_copies = [
        pltpu.make_async_copy(ref, staged.at[i], staged_sems.at[i])
        for i, ref in enumerate((k_hbm, kd_hbm, v_hbm, vd_hbm, q_hbm, qd_hbm))
    ]
    for copy in staged_copies:
        copy.start()
    weight_copies = []
    for j in range(group):
        rows = pl.ds(pl.multiple_of(head_of(j) * HD, HD), HD)
        copy = pltpu.make_async_copy(
            w_hbm.at[rows], weight.at[pl.ds(j * HD, HD)], weight_sem.at[j]
        )
        copy.start()
        weight_copies.append(copy)

    barrier = pltpu.get_barrier_semaphore()
    partners = [taker(j) for j in range(1, group)] + [sibling, right]
    partners += [along_y(way, dx) for way in (0, 1) for dx in range(nx)]
    if nz > 2:
        partners.append(left)
    for partner in partners:
        pl.semaphore_signal(barrier, inc=1, device_id=partner, device_id_type=MESH)

    for copy in staged_copies:
        copy.wait()
    for j in range(group):
        columns = pl.ds(pl.multiple_of(head_of(j) * HD, HD), HD)
        for part in (0, 1):
            send_kv[part, j] = jnp.concatenate(
                [staged[i, :, columns].astype(F32) for i in (2 * part, 2 * part + 1)], axis=0
            ).astype(BF16)
        send_q[j] = jnp.concatenate(
            [staged[i, :, columns].astype(F32) for i in (4, 5)], axis=0
        ).astype(BF16)

    pl.semaphore_wait(barrier, len(partners))

    def remote(src, dst, send_sem, recv_sem, to):
        return pltpu.make_async_remote_copy(
            src_ref=src,
            dst_ref=dst,
            send_sem=send_sem,
            recv_sem=recv_sem,
            device_id=to,
            device_id_type=MESH,
        )

    near_kv = [
        remote(
            send_kv.at[:, j], land_kv.at[:, j], kv_sems.at[0, 0, j], kv_sems.at[1, 0, j], taker(j)
        )
        for j in range(1, nx)
    ]
    near_q = [
        remote(send_q.at[j], land_q.at[j], q_sems.at[0, j], q_sems.at[1, j], taker(j))
        for j in range(1, nx)
    ]
    q_split = ((0, (nx + 1) // 2), ((nx + 1) // 2, nx))
    leg_q, leg_kv, far_q, far_kv = [], [], [], []
    for way in (0, 1):
        low, high = q_split[way]
        leg_kv.append(
            remote(
                send_kv.at[way, pl.ds(nx, nx)],
                relay_kv.at[way],
                relay_kv_sems.at[0, way],
                relay_kv_sems.at[1, way],
                along_y(way, 0),
            )
        )
        far_kv.append(
            [
                remote(
                    relay_kv.at[way, dx],
                    land_kv.at[way, nx + dx],
                    kv_sems.at[0, way, nx + dx],
                    kv_sems.at[1, way, nx + dx],
                    along_y(way, dx),
                )
                for dx in range(nx)
            ]
        )
        if high > low:
            leg_q.append(
                remote(
                    send_q.at[pl.ds(nx + low, high - low)],
                    relay_q.at[pl.ds(low, high - low)],
                    relay_q_sems.at[0, way],
                    relay_q_sems.at[1, way],
                    along_y(way, 0),
                )
            )
            far_q.append(
                [
                    remote(
                        relay_q.at[dx],
                        land_q.at[nx + dx],
                        q_sems.at[0, nx + dx],
                        q_sems.at[1, nx + dx],
                        along_y(way, dx),
                    )
                    for dx in range(low, high)
                ]
            )
    for copy in near_kv + leg_q + leg_kv + near_q:
        copy.start()

    def relay():
        for legs, onward in ((leg_q, far_q), (leg_kv, far_kv)):
            for leg, copies in zip(legs, onward):
                leg.wait_recv()
                for copy in copies:
                    copy.start()

    def slot(way, step):
        if step == 0:
            return half - 1, 0
        if step == half:
            return half - 1, 1
        return step - 1, way

    def steps_of(piece, way):
        return half if (piece == NEAR) == (way == RIGHTWARD) else half - 1

    ring_copies = {}
    part_rows = (pl.ds(0, far_rows // 2), pl.ds(far_rows // 2, far_rows // 2))
    for piece in (NEAR, FAR):
        for way in (LEFTWARD, RIGHTWARD):
            for step in range(1, steps_of(piece, way) + 1):
                for part in range(4):
                    from_p, from_sub = slot(way, step - 1)
                    to_p, to_sub = slot(way, step)
                    ring_copies[piece, way, step, part] = remote(
                        kv.at[piece, from_p, part // 2, from_sub, part_rows[part % 2]],
                        kv.at[piece, to_p, part // 2, to_sub, part_rows[part % 2]],
                        ring_send_sems.at[piece, way, step - 1, part],
                        ring_recv_sems.at[piece, way, step - 1, part],
                        right if way == RIGHTWARD else left,
                    )

    def start_piece(piece):
        members = range(piece * nx, (piece + 1) * nx)
        for copy in near_kv if piece == NEAR else far_kv[0] + far_kv[1]:
            copy.wait_recv()
        for part in (0, 1):
            blocks = [(send_kv if j == 0 else land_kv)[part, j].astype(F32) for j in members]
            for side in (0, 1):
                at = side * tokens
                kv[piece, half - 1, part, 0, :, side * HD : (side + 1) * HD] = jnp.concatenate(
                    [block[at : at + tokens] for block in blocks], axis=0
                ).astype(BF16)
        for part in range(4):
            for way in (RIGHTWARD, LEFTWARD):
                if steps_of(piece, way) >= 1:
                    ring_copies[piece, way, 1, part].start()

    def pass_on(piece, step):
        for part in range(4):
            for way in (RIGHTWARD, LEFTWARD) if piece == NEAR else (LEFTWARD, RIGHTWARD):
                if step <= steps_of(piece, way):
                    ring_copies[piece, way, step, part].wait_recv()
                    if step + 1 <= steps_of(piece, way):
                        ring_copies[piece, way, step + 1, part].start()

    def gather_queries():
        for copies in [near_q] + far_q:
            for copy in copies:
                copy.wait_recv()
        for side, at in ((0, tokens), (1, 0)):
            q_all[:rows_own, side * HD : (side + 1) * HD] = jnp.concatenate(
                [
                    (send_q if j == 0 else land_q)[j].astype(F32)[at : at + tokens]
                    for j in range(group)
                ],
                axis=0,
            ).astype(BF16)

    queries_over = remote(
        q_all.at[pl.ds(0, rows_own)],
        q_all.at[pl.ds(rows_own, rows_own)],
        pair_sems.at[0, 2],
        pair_sems.at[1, 2],
        sibling,
    )
    merge_copies = [
        remote(
            merge_send.at[:, pl.ds(chunk * far_rows, far_rows)],
            merge_land.at[:, pl.ds(chunk * far_rows, far_rows)],
            pair_sems.at[0, chunk],
            pair_sems.at[1, chunk],
            sibling,
        )
        for chunk in (0, 1)
    ]

    def by_lane(block):
        width = block.shape[1]
        whole = width - width % HD
        total = block[:, :HD]
        for at in range(HD, whole, HD):
            total = total + block[:, at : at + HD]
        if width > whole:
            empty = jnp.zeros((block.shape[0], HD - width + whole), F32)
            total = total + jnp.concatenate([block[:, whole:], empty], axis=1)
        return total

    def absorb(piece, p):
        keys = kv[piece, p, 0].reshape(2 * far_rows, 2 * HD)
        vals = kv[piece, p, 1].reshape(2 * far_rows, 2 * HD)
        both = q_all[...]
        transposed = (((1,), (1,)), ((), ()))
        scores = lax.dot_general(
            both[:, HD:], keys[:, :HD], transposed, preferred_element_type=F32
        ) * SCALE
        score_tangent = lax.dot_general(both, keys, transposed, preferred_element_type=F32)
        max_was = row_max[...][:, :1]
        max_now = jnp.maximum(max_was, jnp.max(scores, axis=-1, keepdims=True))
        rescale = jnp.exp(max_was - max_now)
        weights = jnp.exp(scores - max_now).astype(BF16)
        wide = weights.astype(F32)
        shifted = wide * score_tangent
        shaded = shifted.astype(BF16)
        row_max[...] = jnp.broadcast_to(max_now, row_max.shape)
        row_total[...] = row_total[...] * rescale + by_lane(wide)
        tilt_sum[...] = tilt_sum[...] * rescale + by_lane(shifted)
        acc[...] = acc[...] * rescale + jnp.dot(weights, vals, preferred_element_type=F32)
        acc_shaded[...] = acc_shaded[...] * rescale + jnp.dot(
            shaded, vals[:, :HD], preferred_element_type=F32
        )

    row_max[...] = jnp.full(row_max.shape, -1e30, F32)
    row_total[...] = jnp.zeros(row_total.shape, F32)
    tilt_sum[...] = jnp.zeros(tilt_sum.shape, F32)
    acc[...] = jnp.zeros(acc.shape, F32)
    acc_shaded[...] = jnp.zeros(acc_shaded.shape, F32)

    start_piece(NEAR)
    relay()

    before = {at: [] for at in range(2 * half)}
    for step in range(1, min(half, 2) + 1):
        before[0].append((NEAR, step))
    at = 1
    for step in range(1, half + 1):
        if step + 2 <= half:
            before[at].append((NEAR, step + 2))
            at += 1
        before[2 * half - 1 if step == half else at].append((FAR, step))
        at += 1

    def block(at, carry):
        for now, arrivals in before.items():
            if not arrivals:
                continue

            @pl.when(at == now)
            def _(now=now, arrivals=arrivals):
                for piece, step in arrivals:
                    pass_on(piece, step)
                if now == 0:
                    start_piece(FAR)
                    gather_queries()
                    queries_over.start()
                    queries_over.wait_recv()

        piece, p = at // half, at % half
        absorb(piece, p)
        return carry

    lax.fori_loop(0, 2 * half, block, 0)

    out_copies = [
        None
        if j == 0
        else remote(out_send.at[j], out_land.at[j], out_sems.at[0, j], out_sems.at[1, j], giver(j))
        for j in range(group)
    ]

    def state(first):
        rows = slice(first, first + far_rows)
        return (
            acc[rows, :HD],
            acc[rows, HD:] + SCALE * acc_shaded[rows, :],
            row_max[rows, :][:, :1],
            jnp.sum(row_total[rows, :], axis=-1, keepdims=True),
            SCALE * jnp.sum(tilt_sum[rows, :], axis=-1, keepdims=True),
        )

    lane = lax.broadcasted_iota(jnp.int32, (far_rows, HD), 1)
    for chunk in (1, 0):
        rows = slice(chunk * far_rows, (chunk + 1) * far_rows)
        weighted, tangent, top, total, tilt = state(rows_own + chunk * far_rows)
        merge_send[0, rows, :] = weighted
        merge_send[1, rows, :] = tangent
        merge_send[2, rows, :] = jnp.where(lane == 0, top, jnp.where(lane == 1, total, tilt))
        merge_copies[chunk].start()
    for chunk in (1, 0):
        rows = slice(chunk * far_rows, (chunk + 1) * far_rows)
        weighted, tangent, top, total, tilt = state(chunk * far_rows)
        merge_copies[chunk].wait_recv()
        other = merge_land[2, rows, :]
        other_top = other[:, 0:1]
        joint = jnp.maximum(top, other_top)
        mine, theirs = jnp.exp(top - joint), jnp.exp(other_top - joint)
        inverse = 1.0 / (mine * total + theirs * other[:, 1:2])
        mine, theirs = mine * inverse, theirs * inverse
        attended = mine * weighted + theirs * merge_land[0, rows, :]
        tilt = mine * tilt + theirs * other[:, 2:3]
        attended_dot = mine * tangent + theirs * merge_land[1, rows, :] - tilt * attended
        for at in range(nx):
            j = chunk * nx + at
            own = slice(at * tokens, (at + 1) * tokens)
            block = jnp.concatenate([attended[own], attended_dot[own]], axis=0).astype(BF16)
            if j == 0:
                out_land[j] = block
            else:
                out_send[j] = block
                out_copies[j].start()

    for copy in weight_copies:
        copy.wait()
    for j in range(1, group):
        out_copies[j].wait_recv()
    everything = jnp.concatenate([out_land[j] for j in range(group)], axis=1)
    out_ref[...] = jnp.dot(everything, weight[...], preferred_element_type=F32)

    for j in range(1, group):
        out_copies[j].wait_send()
    for copies in [near_kv, near_q, leg_kv, leg_q] + far_kv + far_q:
        for copy in copies:
            copy.wait_send()
    for copy in ring_copies.values():
        copy.wait_send()
    queries_over.wait_send()
    for copy in merge_copies:
        copy.wait_send()


def local(
    queries,
    key_rows,
    values,
    query_tangent,
    key_tangent,
    value_tangent,
    out_weight,
    gate_vector,
    gate_tangent,
    *,
    seq_size,
):
    tokens = queries.shape[0]
    group = queries.shape[1] // HD
    nx = group // 2
    nz = seq_size // nx
    width = out_weight.shape[1]
    rows = group * tokens
    piece_rows = nx * tokens
    half = nz // 2
    vmem = pl.BlockSpec(memory_space=pltpu.VMEM)
    all_rows = rows * nz * 2
    projected = pl.pallas_call(
        functools.partial(kernel, nx, nz),
        out_shape=jax.ShapeDtypeStruct((2 * tokens, width), F32),
        in_specs=[pl.BlockSpec(memory_space=pl.ANY)] * 7,
        out_specs=vmem,
        scratch_shapes=[
            pltpu.VMEM((6, tokens, group * HD), BF16),
            pltpu.VMEM((2, group, 2 * tokens, HD), BF16),
            pltpu.VMEM((group, 2 * tokens, HD), BF16),
            pltpu.VMEM((2, group, 2 * tokens, HD), BF16),
            pltpu.VMEM((group, 2 * tokens, HD), BF16),
            pltpu.VMEM((2, nx, 2 * tokens, HD), BF16),
            pltpu.VMEM((nx, 2 * tokens, HD), BF16),
            pltpu.VMEM((2, half, 2, 2, piece_rows, 2 * HD), BF16),
            pltpu.VMEM((2 * rows, 2 * HD), BF16),
            pltpu.VMEM((2 * rows, 2 * HD), F32),
            pltpu.VMEM((2 * rows, HD), F32),
            pltpu.VMEM((2 * rows, HD), F32),
            pltpu.VMEM((2 * rows, HD), F32),
            pltpu.VMEM((2 * rows, HD), F32),
            pltpu.VMEM((3, rows, HD), F32),
            pltpu.VMEM((3, rows, HD), F32),
            pltpu.VMEM((group, 2 * tokens, HD), BF16),
            pltpu.VMEM((group, 2 * tokens, HD), BF16),
            pltpu.VMEM((group * HD, width), BF16),
            pltpu.SemaphoreType.DMA((6,)),
            pltpu.SemaphoreType.DMA((group,)),
            pltpu.SemaphoreType.DMA((2, 2, group)),
            pltpu.SemaphoreType.DMA((2, group)),
            pltpu.SemaphoreType.DMA((2, 2)),
            pltpu.SemaphoreType.DMA((2, 2)),
            pltpu.SemaphoreType.DMA((2, group)),
            pltpu.SemaphoreType.DMA((2, 2, half, 4)),
            pltpu.SemaphoreType.DMA((2, 2, half, 4)),
            pltpu.SemaphoreType.DMA((2, 3)),
        ],
        compiler_params=pltpu.CompilerParams(
            collective_id=0, has_side_effects=True, vmem_limit_bytes=VMEM_LIMIT
        ),
        cost_estimate=pl.CostEstimate(
            flops=12 * rows * all_rows * HD,
            bytes_accessed=16 * all_rows * HD,
            transcendentals=rows * all_rows,
        ),
    )(
        queries,
        key_rows,
        values,
        query_tangent,
        key_tangent,
        value_tangent,
        out_weight,
    )
    primal, dot = projected[:tokens], projected[tokens:]
    block_out = (gate_vector * primal).astype(BF16)
    block_tangent = (gate_tangent * primal + gate_vector * dot).astype(BF16)
    return block_out, block_tangent


def solution(mesh):
    rows = P(("dp", "seq", "head"), None)
    return jax.shard_map(
        functools.partial(local, seq_size=mesh.shape["seq"]),
        mesh=mesh,
        in_specs=(rows,) * 6 + (P(), P("dp"), P("dp")),
        out_specs=(rows, rows),
        check_vma=False,
    )
```

```python
import functools

import jax
import jax.numpy as jnp
from jax import lax
from jax.experimental import pallas as pl
from jax.experimental.pallas import tpu as pltpu
from jax.sharding import PartitionSpec as P

HD = 128
VMEM_LIMIT = 64 * 1024 * 1024
MESH = pl.DeviceIdType.MESH
SCALE = HD**-0.5
F32 = jnp.float32
BF16 = jnp.bfloat16
NEAR, FAR = 0, 1
LEFTWARD, RIGHTWARD = 0, 1


def kernel(
    nx,
    nz,
    q_hbm,
    k_hbm,
    v_hbm,
    qd_hbm,
    kd_hbm,
    vd_hbm,
    w_hbm,
    out_ref,
    staged,
    send_kv,
    send_q,
    land_kv,
    land_q,
    relay_kv,
    relay_q,
    kv,
    q_all,
    acc,
    acc_shaded,
    row_max,
    row_total,
    out_send,
    out_land,
    weight,
    staged_sems,
    weight_sem,
    kv_sems,
    q_sems,
    relay_kv_sems,
    relay_q_sems,
    out_sems,
    ring_send_sems,
    ring_recv_sems,
    pair_send_sems,
    pair_recv_sems,
):
    tokens = q_hbm.shape[0]
    group = 2 * nx
    far_rows = nx * tokens
    half = nz // 2
    dp = lax.axis_index("dp")
    seq = lax.axis_index("seq")
    head_axis = lax.axis_index("head")
    z, x = seq // nx, seq % nx
    y, core = head_axis // 2, head_axis % 2

    def device(z_at, y_at, x_at, core_at):
        return (dp, z_at * nx + x_at, y_at * 2 + core_at)

    other_dp = (dp + 2) % 4
    other_y = ((y + (dp + 2) // 4) % 2, (y + (dp + 2) // 4 + 1) % 2)

    def along_y(way, dx):
        return (other_dp, z * nx + (x + dx) % nx, other_y[way] * 2 + core)

    def taker(j):
        return device(z, (y + j // nx) % 2, (x + j % nx) % nx, core)

    def giver(j):
        return device(z, (y + j // nx) % 2, (x + nx - j % nx) % nx, core)

    def head_of(j):
        return ((y + j // nx) % 2) * nx + (x + j % nx) % nx

    right = device((z + 1) % nz, y, x, core)
    left = device((z + nz - 1) % nz, y, x, core)
    sibling = device(z, y, x, 1 - core)

    staged_copies = [
        pltpu.make_async_copy(ref, staged.at[i], staged_sems.at[i])
        for i, ref in enumerate((k_hbm, kd_hbm, v_hbm, vd_hbm, q_hbm, qd_hbm))
    ]
    for copy in staged_copies:
        copy.start()
    weight_copies = []
    for j in range(group):
        rows = pl.ds(pl.multiple_of(head_of(j) * HD, HD), HD)
        copy = pltpu.make_async_copy(
            w_hbm.at[rows], weight.at[pl.ds(j * HD, HD)], weight_sem.at[j]
        )
        copy.start()
        weight_copies.append(copy)

    barrier = pltpu.get_barrier_semaphore()
    partners = [taker(j) for j in range(1, group)] + [sibling, right]
    partners += [along_y(way, dx) for way in (0, 1) for dx in range(nx)]
    if nz > 2:
        partners.append(left)
    for partner in partners:
        pl.semaphore_signal(barrier, inc=1, device_id=partner, device_id_type=MESH)

    for copy in staged_copies:
        copy.wait()
    for j in range(group):
        columns = pl.ds(pl.multiple_of(head_of(j) * HD, HD), HD)
        for part in (0, 1):
            send_kv[part, j] = jnp.concatenate(
                [staged[i, :, columns].astype(F32) for i in (2 * part, 2 * part + 1)], axis=0
            ).astype(BF16)
        send_q[j] = jnp.concatenate(
            [staged[i, :, columns].astype(F32) for i in (4, 5)], axis=0
        ).astype(BF16)

    pl.semaphore_wait(barrier, len(partners))

    def remote(src, dst, send_sem, recv_sem, to):
        return pltpu.make_async_remote_copy(
            src_ref=src,
            dst_ref=dst,
            send_sem=send_sem,
            recv_sem=recv_sem,
            device_id=to,
            device_id_type=MESH,
        )

    near_kv = [
        remote(
            send_kv.at[:, j], land_kv.at[:, j], kv_sems.at[0, 0, j], kv_sems.at[1, 0, j], taker(j)
        )
        for j in range(1, nx)
    ]
    near_q = [
        remote(send_q.at[j], land_q.at[j], q_sems.at[0, j], q_sems.at[1, j], taker(j))
        for j in range(1, nx)
    ]
    q_split = ((0, (nx + 1) // 2), ((nx + 1) // 2, nx))
    leg_q, leg_kv, far_q, far_kv = [], [], [], []
    for way in (0, 1):
        low, high = q_split[way]
        leg_kv.append(
            remote(
                send_kv.at[way, pl.ds(nx, nx)],
                relay_kv.at[way],
                relay_kv_sems.at[0, way],
                relay_kv_sems.at[1, way],
                along_y(way, 0),
            )
        )
        far_kv.append(
            [
                remote(
                    relay_kv.at[way, dx],
                    land_kv.at[way, nx + dx],
                    kv_sems.at[0, way, nx + dx],
                    kv_sems.at[1, way, nx + dx],
                    along_y(way, dx),
                )
                for dx in range(nx)
            ]
        )
        if high > low:
            leg_q.append(
                remote(
                    send_q.at[pl.ds(nx + low, high - low)],
                    relay_q.at[pl.ds(low, high - low)],
                    relay_q_sems.at[0, way],
                    relay_q_sems.at[1, way],
                    along_y(way, 0),
                )
            )
            far_q.append(
                [
                    remote(
                        relay_q.at[dx],
                        land_q.at[nx + dx],
                        q_sems.at[0, nx + dx],
                        q_sems.at[1, nx + dx],
                        along_y(way, dx),
                    )
                    for dx in range(low, high)
                ]
            )
    for copy in near_kv + leg_q + leg_kv + near_q:
        copy.start()

    def relay():
        for legs, onward in ((leg_q, far_q), (leg_kv, far_kv)):
            for leg, copies in zip(legs, onward):
                leg.wait_recv()
                for copy in copies:
                    copy.start()

    def slot(way, step):
        if step == 0:
            return half - 1, 0
        if step == half:
            return half - 1, 1
        return step - 1, way

    def steps_of(piece, way):
        return half if (piece == NEAR) == (way == RIGHTWARD) else half - 1

    ring_copies = {}
    part_rows = (pl.ds(0, far_rows // 2), pl.ds(far_rows // 2, far_rows // 2))
    for piece in (NEAR, FAR):
        for way in (LEFTWARD, RIGHTWARD):
            for step in range(1, steps_of(piece, way) + 1):
                for part in range(4):
                    from_p, from_sub = slot(way, step - 1)
                    to_p, to_sub = slot(way, step)
                    ring_copies[piece, way, step, part] = remote(
                        kv.at[piece, from_p, part // 2, from_sub, part_rows[part % 2]],
                        kv.at[piece, to_p, part // 2, to_sub, part_rows[part % 2]],
                        ring_send_sems.at[piece, way, step - 1, part],
                        ring_recv_sems.at[piece, way, step - 1, part],
                        right if way == RIGHTWARD else left,
                    )

    def pair_copy(piece, p, sub):
        return remote(
            kv.at[piece, p, :, sub],
            kv.at[piece, p, :, 2 + sub],
            pair_send_sems.at[piece, p, sub],
            pair_recv_sems.at[piece, p, sub],
            sibling,
        )

    def start_piece(piece):
        members = range(piece * nx, (piece + 1) * nx)
        for copy in near_kv if piece == NEAR else far_kv[0] + far_kv[1]:
            copy.wait_recv()
        for part in (0, 1):
            blocks = [(send_kv if j == 0 else land_kv)[part, j].astype(F32) for j in members]
            for side in (0, 1):
                at = side * tokens
                kv[piece, half - 1, part, 0, :, side * HD : (side + 1) * HD] = jnp.concatenate(
                    [block[at : at + tokens] for block in blocks], axis=0
                ).astype(BF16)
        for part in range(4):
            for way in (RIGHTWARD, LEFTWARD):
                if steps_of(piece, way) >= 1:
                    ring_copies[piece, way, 1, part].start()
        pair_copy(piece, half - 1, 0).start()

    def pass_on(piece, step):
        for part in range(4):
            for way in (RIGHTWARD, LEFTWARD) if piece == NEAR else (LEFTWARD, RIGHTWARD):
                if step <= steps_of(piece, way):
                    ring_copies[piece, way, step, part].wait_recv()
                    if step + 1 <= steps_of(piece, way):
                        ring_copies[piece, way, step + 1, part].start()
                    if part == 3:
                        pair_copy(piece, *slot(way, step)).start()

    def gather_queries():
        for copies in [near_q] + far_q:
            for copy in copies:
                copy.wait_recv()
        for side, at in ((0, tokens), (1, 0)):
            q_all[:, side * HD : (side + 1) * HD] = jnp.concatenate(
                [
                    (send_q if j == 0 else land_q)[j].astype(F32)[at : at + tokens]
                    for j in range(group)
                ],
                axis=0,
            ).astype(BF16)

    def by_lane(block):
        total = block[:, :HD]
        for at in range(HD, block.shape[1], HD):
            total = total + block[:, at : at + HD]
        return total

    def absorb(piece, p):
        keys = kv[piece, p, 0].reshape(4 * far_rows, 2 * HD)
        vals = kv[piece, p, 1].reshape(4 * far_rows, 2 * HD)
        both = q_all[...]
        transposed = (((1,), (1,)), ((), ()))
        scores = SCALE * lax.dot_general(
            both[:, HD:], keys[:, :HD], transposed, preferred_element_type=F32
        )
        score_tangent = lax.dot_general(
            both, keys, transposed, preferred_element_type=F32
        ).astype(BF16)
        max_was = row_max[...]
        max_now = jnp.maximum(max_was, jnp.max(scores, axis=-1, keepdims=True))
        rescale = jnp.exp(max_was - max_now)
        rescale_wide = jnp.concatenate([rescale, rescale], axis=1)
        wide = jnp.exp(scores - jnp.concatenate([max_now] * (scores.shape[1] // HD), axis=1))
        weights = wide.astype(BF16)
        shaded = weights * score_tangent
        row_max[...] = max_now
        row_total[...] = row_total[...] * rescale + by_lane(wide)
        acc[...] = acc[...] * rescale_wide + jnp.dot(
            weights, vals, preferred_element_type=F32
        )
        vals_and_ones = jnp.concatenate([vals[:, :HD], jnp.ones((4 * far_rows, HD), BF16)], axis=1)
        acc_shaded[...] = acc_shaded[...] * rescale_wide + jnp.dot(
            shaded, vals_and_ones, preferred_element_type=F32
        )

    row_max[...] = jnp.full(row_max.shape, -1e30, F32)
    row_total[...] = jnp.zeros(row_total.shape, F32)
    acc[...] = jnp.zeros(acc.shape, F32)
    acc_shaded[...] = jnp.zeros(acc_shaded.shape, F32)

    start_piece(NEAR)
    relay()

    before = {0: [(NEAR, 1)], 1: [(NEAR, 2), (FAR, 0)], 2 * half - 1: [(FAR, half)]}
    if half == 4:
        before |= {2: [(NEAR, 3), (FAR, 1)], 3: [(NEAR, 4)], 4: [(FAR, 2)], 5: [(FAR, 3)]}
    else:
        before[1].append((FAR, 1))

    def block(at, carry):
        for now, arrivals in before.items():

            @pl.when(at == now)
            def _(now=now, arrivals=arrivals):
                for piece, step in arrivals:
                    if step == 0:
                        start_piece(piece)
                    else:
                        pass_on(piece, step)
                if now == 0:
                    gather_queries()

        order = at + jnp.where(at == half - 1, 1, 0) - jnp.where(at == half, 1, 0)
        piece, p = order // half, order % half
        for sub in (0, 1):
            pair_copy(piece, p, sub).wait_recv()
        absorb(piece, p)
        return carry

    lax.fori_loop(0, 2 * half, block, 0)

    out_copies = [
        None
        if j == 0
        else remote(out_send.at[j], out_land.at[j], out_sems.at[0, j], out_sems.at[1, j], giver(j))
        for j in range(group)
    ]
    for chunk in (1, 0):
        rows = slice(chunk * far_rows, (chunk + 1) * far_rows)
        inverse = 1.0 / jnp.sum(row_total[rows, :], axis=-1, keepdims=True)
        tilt = SCALE * acc_shaded[rows, HD:] * inverse
        attended = acc[rows, :HD] * inverse
        tangent = acc[rows, HD:] + SCALE * acc_shaded[rows, :HD]
        attended_dot = tangent * inverse - tilt * attended
        for at in range(nx):
            j = chunk * nx + at
            own = slice(at * tokens, (at + 1) * tokens)
            block = jnp.concatenate([attended[own], attended_dot[own]], axis=0).astype(BF16)
            if j == 0:
                out_land[j] = block
            else:
                out_send[j] = block
                out_copies[j].start()

    for copy in weight_copies:
        copy.wait()
    for j in range(1, group):
        out_copies[j].wait_recv()
    everything = jnp.concatenate([out_land[j] for j in range(group)], axis=1)
    out_ref[...] = jnp.dot(everything, weight[...], preferred_element_type=F32)

    for j in range(1, group):
        out_copies[j].wait_send()
    for copies in [near_kv, near_q, leg_kv, leg_q] + far_kv + far_q:
        for copy in copies:
            copy.wait_send()
    for copy in ring_copies.values():
        copy.wait_send()
    for piece in (NEAR, FAR):
        for p in range(half):
            for sub in (0, 1):
                pair_copy(piece, p, sub).wait_send()


def local(
    queries,
    key_rows,
    values,
    query_tangent,
    key_tangent,
    value_tangent,
    out_weight,
    gate_vector,
    gate_tangent,
    *,
    seq_size,
):
    tokens = queries.shape[0]
    group = queries.shape[1] // HD
    nx = group // 2
    nz = seq_size // nx
    width = out_weight.shape[1]
    rows = group * tokens
    piece_rows = nx * tokens
    half = nz // 2
    vmem = pl.BlockSpec(memory_space=pltpu.VMEM)
    all_rows = rows * nz * 2
    projected = pl.pallas_call(
        functools.partial(kernel, nx, nz),
        out_shape=jax.ShapeDtypeStruct((2 * tokens, width), F32),
        in_specs=[pl.BlockSpec(memory_space=pl.ANY)] * 7,
        out_specs=vmem,
        scratch_shapes=[
            pltpu.VMEM((6, tokens, group * HD), BF16),
            pltpu.VMEM((2, group, 2 * tokens, HD), BF16),
            pltpu.VMEM((group, 2 * tokens, HD), BF16),
            pltpu.VMEM((2, group, 2 * tokens, HD), BF16),
            pltpu.VMEM((group, 2 * tokens, HD), BF16),
            pltpu.VMEM((2, nx, 2 * tokens, HD), BF16),
            pltpu.VMEM((nx, 2 * tokens, HD), BF16),
            pltpu.VMEM((2, half, 2, 4, piece_rows, 2 * HD), BF16),
            pltpu.VMEM((rows, 2 * HD), BF16),
            pltpu.VMEM((rows, 2 * HD), F32),
            pltpu.VMEM((rows, 2 * HD), F32),
            pltpu.VMEM((rows, HD), F32),
            pltpu.VMEM((rows, HD), F32),
            pltpu.VMEM((group, 2 * tokens, HD), BF16),
            pltpu.VMEM((group, 2 * tokens, HD), BF16),
            pltpu.VMEM((group * HD, width), BF16),
            pltpu.SemaphoreType.DMA((6,)),
            pltpu.SemaphoreType.DMA((group,)),
            pltpu.SemaphoreType.DMA((2, 2, group)),
            pltpu.SemaphoreType.DMA((2, group)),
            pltpu.SemaphoreType.DMA((2, 2)),
            pltpu.SemaphoreType.DMA((2, 2)),
            pltpu.SemaphoreType.DMA((2, group)),
            pltpu.SemaphoreType.DMA((2, 2, half, 4)),
            pltpu.SemaphoreType.DMA((2, 2, half, 4)),
            pltpu.SemaphoreType.DMA((2, half, 2)),
            pltpu.SemaphoreType.DMA((2, half, 2)),
        ],
        compiler_params=pltpu.CompilerParams(
            collective_id=0, has_side_effects=True, vmem_limit_bytes=VMEM_LIMIT
        ),
        cost_estimate=pl.CostEstimate(
            flops=12 * rows * all_rows * HD,
            bytes_accessed=16 * all_rows * HD,
            transcendentals=rows * all_rows,
        ),
    )(
        queries,
        key_rows,
        values,
        query_tangent,
        key_tangent,
        value_tangent,
        out_weight,
    )
    primal, dot = projected[:tokens], projected[tokens:]
    block_out = (gate_vector * primal).astype(BF16)
    block_tangent = (gate_tangent * primal + gate_vector * dot).astype(BF16)
    return block_out, block_tangent


def solution(mesh):
    rows = P(("dp", "seq", "head"), None)
    return jax.shard_map(
        functools.partial(local, seq_size=mesh.shape["seq"]),
        mesh=mesh,
        in_specs=(rows,) * 6 + (P(), P("dp"), P("dp")),
        out_specs=(rows, rows),
        check_vma=False,
    )
```

```python
import functools

import jax
import jax.numpy as jnp
from jax import lax
from jax.experimental import pallas as pl
from jax.experimental.pallas import tpu as pltpu
from jax.sharding import PartitionSpec as P

HD = 128
VMEM_LIMIT = 64 * 1024 * 1024
MESH = pl.DeviceIdType.MESH
SCALE = HD**-0.5
F32 = jnp.float32
BF16 = jnp.bfloat16
NEAR, FAR = 0, 1
LEFTWARD, RIGHTWARD = 0, 1


def kernel(
    nx,
    nz,
    q_hbm,
    k_hbm,
    v_hbm,
    qd_hbm,
    kd_hbm,
    vd_hbm,
    w_hbm,
    out_ref,
    staged,
    send_kv,
    send_q,
    land_kv,
    land_q,
    relay_kv,
    relay_q,
    kv,
    q_all,
    acc,
    acc_shaded,
    row_max,
    row_total,
    out_send,
    out_land,
    out_relayed,
    weight,
    staged_sems,
    weight_sem,
    kv_sems,
    q_sems,
    relay_kv_sems,
    relay_q_sems,
    out_sems,
    out_leg_sems,
    ring_send_sems,
    ring_recv_sems,
    pair_send_sems,
    pair_recv_sems,
):
    tokens = q_hbm.shape[0]
    group = 2 * nx
    far_rows = nx * tokens
    half = nz // 2
    dp = lax.axis_index("dp")
    seq = lax.axis_index("seq")
    head_axis = lax.axis_index("head")
    z, x = seq // nx, seq % nx
    y, core = head_axis // 2, head_axis % 2

    def device(z_at, y_at, x_at, core_at):
        return (dp, z_at * nx + x_at, y_at * 2 + core_at)

    other_dp = (dp + 2) % 4
    other_y = ((y + (dp + 2) // 4) % 2, (y + (dp + 2) // 4 + 1) % 2)

    def along_y(way, dx):
        return (other_dp, z * nx + (x + dx) % nx, other_y[way] * 2 + core)

    def taker(j):
        return device(z, (y + j // nx) % 2, (x + j % nx) % nx, core)

    def giver(j):
        return device(z, (y + j // nx) % 2, (x + nx - j % nx) % nx, core)

    def head_of(j):
        return ((y + j // nx) % 2) * nx + (x + j % nx) % nx

    right = device((z + 1) % nz, y, x, core)
    left = device((z + nz - 1) % nz, y, x, core)
    sibling = device(z, y, x, 1 - core)

    staged_copies = [
        pltpu.make_async_copy(ref, staged.at[i], staged_sems.at[i])
        for i, ref in enumerate((k_hbm, kd_hbm, v_hbm, vd_hbm, q_hbm, qd_hbm))
    ]
    for copy in staged_copies:
        copy.start()
    weight_copies = []
    for j in range(group):
        rows = pl.ds(pl.multiple_of(head_of(j) * HD, HD), HD)
        copy = pltpu.make_async_copy(
            w_hbm.at[rows], weight.at[pl.ds(j * HD, HD)], weight_sem.at[j]
        )
        copy.start()
        weight_copies.append(copy)

    barrier = pltpu.get_barrier_semaphore()
    partners = [taker(j) for j in range(1, group)] + [sibling, right]
    partners += [along_y(way, dx) for way in (0, 1) for dx in range(nx)]
    if nz > 2:
        partners.append(left)
    for partner in partners:
        pl.semaphore_signal(barrier, inc=1, device_id=partner, device_id_type=MESH)

    for copy in staged_copies:
        copy.wait()
    for j in range(group):
        columns = pl.ds(pl.multiple_of(head_of(j) * HD, HD), HD)
        for part in (0, 1):
            send_kv[part, j] = jnp.concatenate(
                [staged[i, :, columns].astype(F32) for i in (2 * part, 2 * part + 1)], axis=0
            ).astype(BF16)
        send_q[j] = jnp.concatenate(
            [staged[i, :, columns].astype(F32) for i in (4, 5)], axis=0
        ).astype(BF16)

    pl.semaphore_wait(barrier, len(partners))

    def remote(src, dst, send_sem, recv_sem, to):
        return pltpu.make_async_remote_copy(
            src_ref=src,
            dst_ref=dst,
            send_sem=send_sem,
            recv_sem=recv_sem,
            device_id=to,
            device_id_type=MESH,
        )

    near_kv = [
        remote(
            send_kv.at[:, j], land_kv.at[:, j], kv_sems.at[0, 0, j], kv_sems.at[1, 0, j], taker(j)
        )
        for j in range(1, nx)
    ]
    near_q = [
        remote(send_q.at[j], land_q.at[j], q_sems.at[0, j], q_sems.at[1, j], taker(j))
        for j in range(1, nx)
    ]
    q_split = ((0, (nx + 1) // 2), ((nx + 1) // 2, nx))
    leg_q, leg_kv, far_q, far_kv = [], [], [], []
    for way in (0, 1):
        low, high = q_split[way]
        leg_kv.append(
            remote(
                send_kv.at[way, pl.ds(nx, nx)],
                relay_kv.at[way],
                relay_kv_sems.at[0, way],
                relay_kv_sems.at[1, way],
                along_y(way, 0),
            )
        )
        far_kv.append(
            [
                remote(
                    relay_kv.at[way, dx],
                    land_kv.at[way, nx + dx],
                    kv_sems.at[0, way, nx + dx],
                    kv_sems.at[1, way, nx + dx],
                    along_y(way, dx),
                )
                for dx in range(nx)
            ]
        )
        if high > low:
            leg_q.append(
                remote(
                    send_q.at[pl.ds(nx + low, high - low)],
                    relay_q.at[pl.ds(low, high - low)],
                    relay_q_sems.at[0, way],
                    relay_q_sems.at[1, way],
                    along_y(way, 0),
                )
            )
            far_q.append(
                [
                    remote(
                        relay_q.at[dx],
                        land_q.at[nx + dx],
                        q_sems.at[0, nx + dx],
                        q_sems.at[1, nx + dx],
                        along_y(way, dx),
                    )
                    for dx in range(low, high)
                ]
            )
    far_first = sorted(range(1, nx), key=lambda j: -min(j, nx - j))
    for copy in [near_kv[j - 1] for j in far_first] + leg_q + leg_kv + near_q:
        copy.start()

    def relay():
        for legs, onward in ((leg_q, far_q), (leg_kv, far_kv)):
            for leg, copies in zip(legs, onward):
                leg.wait_recv()
                for copy in copies:
                    copy.start()

    def slot(way, step):
        if step == 0:
            return half - 1, 0
        if step == half:
            return half - 1, 1
        return step - 1, way

    def steps_of(piece, way):
        return half if (piece == NEAR) == (way == RIGHTWARD) else half - 1

    ring_copies = {}
    part_rows = (pl.ds(0, far_rows // 2), pl.ds(far_rows // 2, far_rows // 2))
    for piece in (NEAR, FAR):
        for way in (LEFTWARD, RIGHTWARD):
            for step in range(1, steps_of(piece, way) + 1):
                for part in range(4):
                    from_p, from_sub = slot(way, step - 1)
                    to_p, to_sub = slot(way, step)
                    ring_copies[piece, way, step, part] = remote(
                        kv.at[piece, from_p, part // 2, from_sub, part_rows[part % 2]],
                        kv.at[piece, to_p, part // 2, to_sub, part_rows[part % 2]],
                        ring_send_sems.at[piece, way, step - 1, part],
                        ring_recv_sems.at[piece, way, step - 1, part],
                        right if way == RIGHTWARD else left,
                    )

    def pair_copy(piece, p, sub):
        return remote(
            kv.at[piece, p, :, sub],
            kv.at[piece, p, :, 2 + sub],
            pair_send_sems.at[piece, p, sub],
            pair_recv_sems.at[piece, p, sub],
            sibling,
        )

    def start_piece(piece):
        members = range(piece * nx, (piece + 1) * nx)
        for copy in near_kv if piece == NEAR else far_kv[0] + far_kv[1]:
            copy.wait_recv()
        for part in (0, 1):
            blocks = [(send_kv if j == 0 else land_kv)[part, j].astype(F32) for j in members]
            for side in (0, 1):
                at = side * tokens
                kv[piece, half - 1, part, 0, :, side * HD : (side + 1) * HD] = jnp.concatenate(
                    [block[at : at + tokens] for block in blocks], axis=0
                ).astype(BF16)
        for part in range(4):
            for way in (RIGHTWARD, LEFTWARD):
                if steps_of(piece, way) >= 1:
                    ring_copies[piece, way, 1, part].start()
        pair_copy(piece, half - 1, 0).start()

    def pass_on(piece, step):
        for part in range(4):
            for way in (RIGHTWARD, LEFTWARD) if piece == NEAR else (LEFTWARD, RIGHTWARD):
                if step <= steps_of(piece, way):
                    ring_copies[piece, way, step, part].wait_recv()
                    if step + 1 <= steps_of(piece, way):
                        ring_copies[piece, way, step + 1, part].start()
                    if part == 3:
                        pair_copy(piece, *slot(way, step)).start()

    def gather_queries():
        for copies in [near_q] + far_q:
            for copy in copies:
                copy.wait_recv()
        for side, at in ((0, tokens), (1, 0)):
            q_all[:, side * HD : (side + 1) * HD] = jnp.concatenate(
                [
                    (send_q if j == 0 else land_q)[j].astype(F32)[at : at + tokens]
                    for j in range(group)
                ],
                axis=0,
            ).astype(BF16)

    def by_lane(block):
        total = block[:, :HD]
        for at in range(HD, block.shape[1], HD):
            total = total + block[:, at : at + HD]
        return total

    def absorb(piece, p, first, count):
        rows = slice(first, first + count)
        keys = kv[piece, p, 0].reshape(4 * far_rows, 2 * HD)
        vals = kv[piece, p, 1].reshape(4 * far_rows, 2 * HD)
        both = q_all[rows, :]
        transposed = (((1,), (1,)), ((), ()))
        scores = SCALE * lax.dot_general(
            both[:, HD:], keys[:, :HD], transposed, preferred_element_type=F32
        )
        score_tangent = lax.dot_general(
            both, keys, transposed, preferred_element_type=F32
        ).astype(BF16)
        max_was = row_max[rows, :]
        max_now = jnp.maximum(max_was, jnp.max(scores, axis=-1, keepdims=True))
        rescale = jnp.exp(max_was - max_now)
        rescale_wide = jnp.concatenate([rescale, rescale], axis=1)
        wide = jnp.exp(scores - jnp.concatenate([max_now] * (scores.shape[1] // HD), axis=1))
        weights = wide.astype(BF16)
        shaded = weights * score_tangent
        row_max[rows, :] = max_now
        row_total[rows, :] = row_total[rows, :] * rescale + by_lane(wide)
        acc[rows, :] = acc[rows, :] * rescale_wide + jnp.dot(
            weights, vals, preferred_element_type=F32
        )
        vals_and_ones = jnp.concatenate([vals[:, :HD], jnp.ones((4 * far_rows, HD), BF16)], axis=1)
        acc_shaded[rows, :] = acc_shaded[rows, :] * rescale_wide + jnp.dot(
            shaded, vals_and_ones, preferred_element_type=F32
        )

    row_max[...] = jnp.full(row_max.shape, -1e30, F32)
    row_total[...] = jnp.zeros(row_total.shape, F32)
    acc[...] = jnp.zeros(acc.shape, F32)
    acc_shaded[...] = jnp.zeros(acc_shaded.shape, F32)

    start_piece(NEAR)
    relay()

    before = {0: [(NEAR, 1)], 1: [(NEAR, 2), (FAR, 0)]}
    if half == 4:
        before |= {2: [(NEAR, 3), (FAR, 1)], 3: [(NEAR, 4)], 4: [(FAR, 2)], 5: [(FAR, 3)]}
    else:
        before[1].append((FAR, 1))

    def block(at, carry):
        for now, arrivals in before.items():

            @pl.when(at == now)
            def _(now=now, arrivals=arrivals):
                for piece, step in arrivals:
                    if step == 0:
                        start_piece(piece)
                    else:
                        pass_on(piece, step)
                if now == 0:
                    gather_queries()

        order = at + jnp.where(at == half - 1, 1, 0) - jnp.where(at == half, 1, 0)
        piece, p = order // half, order % half
        for sub in (0, 1):
            pair_copy(piece, p, sub).wait_recv()
        absorb(piece, p, 0, 2 * far_rows)
        return carry

    lax.fori_loop(0, 2 * half - 1, block, 0)
    pass_on(FAR, half)
    for sub in (0, 1):
        pair_copy(FAR, half - 1, sub).wait_recv()

    out_near = [
        remote(out_send.at[j], out_land.at[j], out_sems.at[0, j], out_sems.at[1, j], giver(j))
        for j in range(1, nx)
    ]
    out_legs, out_onward = [], []
    for way, (low, high) in enumerate(q_split):
        if high > low:
            out_legs.append(
                remote(
                    out_send.at[pl.ds(nx + low, high - low)],
                    out_relayed.at[pl.ds(low, high - low)],
                    out_leg_sems.at[0, way],
                    out_leg_sems.at[1, way],
                    along_y(way, 0),
                )
            )
            out_onward.append(
                [
                    remote(
                        out_relayed.at[dx],
                        out_land.at[nx + dx],
                        out_sems.at[0, nx + dx],
                        out_sems.at[1, nx + dx],
                        along_y(way, nx - dx),
                    )
                    for dx in range(low, high)
                ]
            )
    for chunk in (1, 0):
        absorb(FAR, half - 1, chunk * far_rows, far_rows)
        rows = slice(chunk * far_rows, (chunk + 1) * far_rows)
        inverse = 1.0 / jnp.sum(row_total[rows, :], axis=-1, keepdims=True)
        tilt = SCALE * acc_shaded[rows, HD:] * inverse
        attended = acc[rows, :HD] * inverse
        tangent = acc[rows, HD:] + SCALE * acc_shaded[rows, :HD]
        attended_dot = tangent * inverse - tilt * attended
        for at in range(nx):
            j = chunk * nx + at
            own = slice(at * tokens, (at + 1) * tokens)
            block = jnp.concatenate([attended[own], attended_dot[own]], axis=0).astype(BF16)
            if j == 0:
                out_land[j] = block
            else:
                out_send[j] = block
        for copy in out_legs if chunk == 1 else out_near:
            copy.start()
    for leg, copies in zip(out_legs, out_onward):
        leg.wait_recv()
        for copy in copies:
            copy.start()

    for copy in weight_copies:
        copy.wait()
    split = nx * HD
    for copy in out_near:
        copy.wait_recv()
    near_heads = jnp.concatenate([out_land[j] for j in range(nx)], axis=1)
    out_ref[...] = jnp.dot(near_heads, weight[:split, :], preferred_element_type=F32)
    for copies in out_onward:
        for copy in copies:
            copy.wait_recv()
    far_heads = jnp.concatenate([out_land[j] for j in range(nx, group)], axis=1)
    out_ref[...] += jnp.dot(far_heads, weight[split:, :], preferred_element_type=F32)

    for copies in [near_kv, near_q, leg_kv, leg_q, out_near, out_legs] + far_kv + far_q + out_onward:
        for copy in copies:
            copy.wait_send()
    for copy in ring_copies.values():
        copy.wait_send()
    for piece in (NEAR, FAR):
        for p in range(half):
            for sub in (0, 1):
                pair_copy(piece, p, sub).wait_send()


def local(
    queries,
    key_rows,
    values,
    query_tangent,
    key_tangent,
    value_tangent,
    out_weight,
    gate_vector,
    gate_tangent,
    *,
    seq_size,
):
    tokens = queries.shape[0]
    group = queries.shape[1] // HD
    nx = group // 2
    nz = seq_size // nx
    width = out_weight.shape[1]
    rows = group * tokens
    piece_rows = nx * tokens
    half = nz // 2
    vmem = pl.BlockSpec(memory_space=pltpu.VMEM)
    all_rows = rows * nz * 2
    projected = pl.pallas_call(
        functools.partial(kernel, nx, nz),
        out_shape=jax.ShapeDtypeStruct((2 * tokens, width), F32),
        in_specs=[pl.BlockSpec(memory_space=pl.ANY)] * 7,
        out_specs=vmem,
        scratch_shapes=[
            pltpu.VMEM((6, tokens, group * HD), BF16),
            pltpu.VMEM((2, group, 2 * tokens, HD), BF16),
            pltpu.VMEM((group, 2 * tokens, HD), BF16),
            pltpu.VMEM((2, group, 2 * tokens, HD), BF16),
            pltpu.VMEM((group, 2 * tokens, HD), BF16),
            pltpu.VMEM((2, nx, 2 * tokens, HD), BF16),
            pltpu.VMEM((nx, 2 * tokens, HD), BF16),
            pltpu.VMEM((2, half, 2, 4, piece_rows, 2 * HD), BF16),
            pltpu.VMEM((rows, 2 * HD), BF16),
            pltpu.VMEM((rows, 2 * HD), F32),
            pltpu.VMEM((rows, 2 * HD), F32),
            pltpu.VMEM((rows, HD), F32),
            pltpu.VMEM((rows, HD), F32),
            pltpu.VMEM((group, 2 * tokens, HD), BF16),
            pltpu.VMEM((group, 2 * tokens, HD), BF16),
            pltpu.VMEM((nx, 2 * tokens, HD), BF16),
            pltpu.VMEM((group * HD, width), BF16),
            pltpu.SemaphoreType.DMA((6,)),
            pltpu.SemaphoreType.DMA((group,)),
            pltpu.SemaphoreType.DMA((2, 2, group)),
            pltpu.SemaphoreType.DMA((2, group)),
            pltpu.SemaphoreType.DMA((2, 2)),
            pltpu.SemaphoreType.DMA((2, 2)),
            pltpu.SemaphoreType.DMA((2, group)),
            pltpu.SemaphoreType.DMA((2, 2)),
            pltpu.SemaphoreType.DMA((2, 2, half, 4)),
            pltpu.SemaphoreType.DMA((2, 2, half, 4)),
            pltpu.SemaphoreType.DMA((2, half, 2)),
            pltpu.SemaphoreType.DMA((2, half, 2)),
        ],
        compiler_params=pltpu.CompilerParams(
            collective_id=0, has_side_effects=True, vmem_limit_bytes=VMEM_LIMIT
        ),
        cost_estimate=pl.CostEstimate(
            flops=12 * rows * all_rows * HD,
            bytes_accessed=16 * all_rows * HD,
            transcendentals=rows * all_rows,
        ),
    )(
        queries,
        key_rows,
        values,
        query_tangent,
        key_tangent,
        value_tangent,
        out_weight,
    )
    primal, dot = projected[:tokens], projected[tokens:]
    block_out = (gate_vector * primal).astype(BF16)
    block_tangent = (gate_tangent * primal + gate_vector * dot).astype(BF16)
    return block_out, block_tangent


def solution(mesh):
    rows = P(("dp", "seq", "head"), None)
    return jax.shard_map(
        functools.partial(local, seq_size=mesh.shape["seq"]),
        mesh=mesh,
        in_specs=(rows,) * 6 + (P(), P("dp"), P("dp")),
        out_specs=(rows, rows),
        check_vma=False,
    )
```
